128 devices in a mesh: ctx: 32 (over y, z, x_lo), tp: 4 (over x_hi, core).
Axes of the slice: x: 4 (x_hi: 2, x_lo: 2; x = x_hi * 2 + x_lo), y: 4, z: 4, core: 2. Of those that a mesh axis runs over, the one named last changes fastest.
Arguments:
- residual: bfloat16 [8192, 5120], P('ctx'), may hold values from -24 to 24
- out_grad: bfloat16 [8192, 5120], P('ctx'), may hold values from -6 to 6
- queries: bfloat16 [8192, 2560], P('ctx', 'tp'), may hold values from -6 to 6
- key_rows: bfloat16 [8192, 512], P('ctx', 'tp'), may hold values from -6 to 6
- value_rows: bfloat16 [8192, 512], P('ctx', 'tp'), may hold values from -6 to 6
- doc_ids: int32 [8192], P('ctx'), may hold values from 0 to 7, never falling along the last dimension, each value on 1 to 6144 neighbouring positions
- expert_ids: int32 [8192], P('ctx'), may hold values from 0 to 127, as said below
- norm_gain: bfloat16 [5120], replicated, may hold values from 0.099609375 to 1.8984375
- router_columns: bfloat16 [5120, 4], P(None, 'tp'), may hold values from -0.078125 to 0.078125
- gate_weight: bfloat16 [4, 5120, 8192], P('tp', None, 'ctx'), may hold values from -0.15625 to 0.15625
- up_weight: bfloat16 [4, 5120, 8192], P('tp', None, 'ctx'), may hold values from -0.15625 to 0.15625
- down_weight: bfloat16 [4, 8192, 5120], P('tp', 'ctx'), may hold values from -0.09375 to 0.09375
- out_weight: bfloat16 [2560, 5120], P('tp', 'ctx'), may hold values from -0.125 to 0.125
Outputs:
- residual_grad: bfloat16 [8192, 5120], P('ctx')
- query_grad: bfloat16 [8192, 2560], P('ctx', 'tp')
- key_grad: bfloat16 [8192, 512], P('ctx', 'tp')
- value_grad: bfloat16 [8192, 512], P('ctx', 'tp')
- grad_gate: bfloat16 [4, 5120, 8192], P('tp', None, 'ctx')
- grad_up: bfloat16 [4, 5120, 8192], P('tp', None, 'ctx')
- grad_down: bfloat16 [4, 8192, 5120], P('tp', 'ctx')
The draws below stay inside these ranges and needn't reach their ends.
Inputs may be any that keep to these rules, and one draw needn't show every extreme that they name: `expert_ids`: in each aligned block of 256 tokens at most 4 tokens name any one expert below 4, and some expert below 4 is named exactly 4 times in every block. `doc_ids`: document numbers never fall along the sequence.
All inputs are finite; a program needn't handle non-finite values.
Results may differ from the reference program's by a relative error of at most 0.03.
Values may be sent and summed in bfloat16 or wider, within the bound.
A program may use at most 128 MiB of HBM per device.

```python
import math
import jax
import jax.numpy as jnp
import numpy as np
from jax import lax

D = 5120
HD = 128
FF = 8192
EXPERTS = 128
HQW = 20
HKVW = 4
SEQ_DEV = 256
CAPL = 4
DOCS = 8
IN_FLIGHT = 4
LEN = 8192


def draw_queries(key, part):
    key = jax.random.fold_in(key, 1)
    return jnp.clip(jax.random.normal(key, (LEN, HQW * HD)), -4.0, 4.0).astype(jnp.bfloat16)


def draw_key_rows(key, part):
    key = jax.random.fold_in(key, 2)
    return jnp.clip(jax.random.normal(key, (LEN, HKVW * HD)), -4.0, 4.0).astype(jnp.bfloat16)


def draw_residual(key, part):
    key = jax.random.fold_in(key, 3)
    first, second, third = jax.random.split(key, 3)
    base = jnp.clip(jax.random.normal(first, (LEN, D)), -4.0, 4.0)
    rows = jnp.exp(jax.random.uniform(second, (LEN, 1), minval=math.log(0.25), maxval=math.log(4.0)))
    columns = jnp.exp(jax.random.uniform(third, (1, D), minval=math.log(2.0 / 3.0), maxval=math.log(1.5)))
    return (base * rows * columns).astype(jnp.bfloat16)


def draw_expert_ids(key, part):
    key = jax.random.fold_in(key, 4)
    blocks = LEN // SEQ_DEV
    first, second, third, fourth = jax.random.split(key, 4)
    counts = jax.random.randint(first, (blocks, IN_FLIGHT), 0, CAPL + 1)
    fullest = jax.random.randint(second, (), 0, IN_FLIGHT)
    counts = jnp.where(jnp.arange(IN_FLIGHT)[None, :] == fullest, CAPL, counts)
    ends = jnp.cumsum(counts, axis=1)
    rank = jnp.arange(SEQ_DEV)
    which = jnp.sum((rank[None, :, None] >= ends[:, None, :]).astype(jnp.int32), axis=2)
    other = jax.random.randint(third, (blocks, SEQ_DEV), IN_FLIGHT, EXPERTS)
    other = other.at[:, SEQ_DEV - 1].set(EXPERTS - 1)
    labels = jnp.where(which < IN_FLIGHT, which, other)
    block_keys = jax.random.split(fourth, blocks)
    orders = jax.vmap(lambda single: jax.random.permutation(single, SEQ_DEV))(block_keys)
    shuffled = jnp.take_along_axis(labels, orders, axis=1)
    return shuffled.reshape(LEN).astype(jnp.int32)


def steps_of(own_key, shape, pieces, least, top_value):
    def one(axis_at, shards_of):
        steps = jax.random.uniform(jax.random.fold_in(jax.random.fold_in(own_key, 6), axis_at), (shards_of,), jnp.float32, least / len(pieces), top_value / len(pieces))
        return jnp.repeat(jnp.exp(steps), shape[axis_at] // shards_of).reshape((-1,) + (1,) * (len(shape) - axis_at - 1))

    loudness = one(*pieces[0])
    for cut in pieces[1:]:
        loudness = loudness * one(*cut)
    return loudness


def split_up(amount, total, bound, slope):
    loads = [(1 << 20) // math.isqrt(grade ** slope) + 1 for grade in range(2, amount + 1)]
    surplus, given = total - bound - (amount - 1), [1] * (amount - 1)
    while surplus > 0:
        candidates = [i for i in range(amount - 1) if given[i] < bound]
        whole, remaining = sum([loads[i] for i in candidates]), surplus
        for i in candidates:
            addition = min(bound - given[i], max(1, remaining * loads[i] // whole), surplus)
            given[i] = given[i] + addition
            surplus = surplus - addition
    return np.array([bound] + given)


def ragged(rng, amount, total, most, lean):
    if amount == 2:
        one = jax.random.randint(rng, (), max(1, total - most), min(most, total - 1) + 1)
        return jnp.stack([one, total - one])
    lengths = jnp.asarray(split_up(amount, total, most, lean), jnp.int32)
    pairs = (amount - 1) // 2
    source_of, receiver = lengths[1:1 + 2 * pairs:2], lengths[2:2 + 2 * pairs:2]
    slack = jnp.minimum(source_of - 1, most - receiver)
    moved = jax.random.randint(jax.random.fold_in(rng, 1), (pairs,), 0, 1 << 20) % (slack + 1)
    lengths = lengths.at[1:1 + 2 * pairs:2].set(source_of - moved).at[2:2 + 2 * pairs:2].set(receiver + moved)
    return lengths[jax.random.permutation(jax.random.fold_in(rng, 2), amount)]


def normal_values(rng, dims, scale, bound, pieces=(), kind=jnp.bfloat16):
    drawn = jax.random.normal(rng, dims, jnp.float32) * scale
    if len(pieces) > 0:
        drawn = steps_of(rng, dims, pieces, -0.22, 0.18) * drawn
    return jnp.clip(drawn, min=-bound, max=bound).astype(kind)


def setup_inputs(seed: int = 0) -> dict:
    arg_keys = jax.random.split(jax.random.key(seed), 14)
    return {
        "residual": draw_residual(jax.random.fold_in(arg_keys[13], 71), 0),
        "out_grad": normal_values(arg_keys[1], (LEN, D), 1.0, 6.0, ((0, 32),)),
        "queries": draw_queries(jax.random.fold_in(arg_keys[13], 71), 0),
        "key_rows": draw_key_rows(jax.random.fold_in(arg_keys[13], 71), 0),
        "value_rows": normal_values(arg_keys[4], (LEN, HKVW * HD), 1.0, 6.0, ((0, 32), (1, 4))),
        "doc_ids": jnp.searchsorted(jnp.cumsum(ragged(arg_keys[5], DOCS, LEN, 3 * LEN // 4, 2)), jnp.arange(LEN), side="right").astype(jnp.int32),
        "expert_ids": draw_expert_ids(jax.random.fold_in(arg_keys[13], 71), 0),
        "norm_gain": jnp.clip(1.0 + 0.18 * jax.random.normal(arg_keys[7], (D,), jnp.float32), 0.099609375, 1.8984375).astype(jnp.bfloat16),
        "router_columns": normal_values(arg_keys[8], (D, IN_FLIGHT), D ** -0.5, 0.078125, ((1, 4),)),
        "gate_weight": normal_values(arg_keys[9], (IN_FLIGHT, D, FF), (D // 4) ** -0.5, 0.15625, ((0, 4), (2, 32))),
        "up_weight": normal_values(arg_keys[10], (IN_FLIGHT, D, FF), (D // 4) ** -0.5, 0.15625, ((0, 4), (2, 32))),
        "down_weight": normal_values(arg_keys[11], (IN_FLIGHT, FF, D), (FF // 2) ** -0.5, 0.09375, ((0, 4), (1, 32))),
        "out_weight": normal_values(arg_keys[12], (HQW * HD, D), (HQW * HD) ** -0.5, 0.125, ((0, 4), (1, 32))),
    }


EPS = 1e-05
NEG = -1e+30

def held(value):
    return lax.optimization_barrier(value.astype(jnp.bfloat16)).astype(jnp.float32)

def expert_part(residual, out_grad, expert_ids, norm_gain, router_columns, gate_weight, up_weight, down_weight):
    blocks = LEN // SEQ_DEV
    total_rows = blocks * CAPL
    hidden = residual.astype(jnp.float32)
    inverse = lax.rsqrt(lax.optimization_barrier(jnp.mean(hidden * hidden, axis=1, keepdims=True)) + EPS)
    gain = norm_gain.astype(jnp.float32)
    normed = (hidden * inverse * gain).astype(jnp.bfloat16)
    token = jnp.arange(LEN, dtype=jnp.int32)
    moe_grad = jnp.zeros((LEN, D), jnp.float32)
    gate_list, up_list, down_list = ([], [], [])
    for expert in range(IN_FLIGHT):
        member = (expert_ids == expert).astype(jnp.int32)
        within = member.reshape(blocks, SEQ_DEV)
        rank = (jnp.cumsum(within, axis=1) - within).reshape(LEN).astype(jnp.int32)
        target = jnp.where(member > 0, token // SEQ_DEV * CAPL + rank, total_rows).astype(jnp.int32)
        source = jnp.zeros((total_rows,), jnp.int32).at[target].set(token, mode='drop')
        filled = jnp.zeros((total_rows,), jnp.float32).at[target].set(1.0, mode='drop')
        live = filled[:, None] > 0.5
        rows_norm = jnp.where(live, normed[source], jnp.zeros((), jnp.bfloat16))
        rows_hidden = jnp.where(live, hidden[source], 0.0)
        rows_inverse = inverse[source]
        rows_grad = jnp.where(live, out_grad[source], jnp.zeros((), jnp.bfloat16))
        column = router_columns[:, expert]
        score = jax.nn.sigmoid(jnp.dot(rows_norm, column, preferred_element_type=jnp.float32))[:, None]
        routed = (rows_norm.astype(jnp.float32) * score).astype(jnp.bfloat16)
        gate = jnp.dot(routed, gate_weight[expert], preferred_element_type=jnp.float32)
        upward = jnp.dot(routed, up_weight[expert], preferred_element_type=jnp.float32)
        sigma = jax.nn.sigmoid(gate)
        swish = gate * sigma
        active = (swish * upward).astype(jnp.bfloat16)
        active_grad = jnp.dot(rows_grad, down_weight[expert].T, preferred_element_type=jnp.float32)
        gate_delta = (active_grad * upward * sigma * (1.0 + gate * (1.0 - sigma))).astype(jnp.bfloat16)
        up_delta = (active_grad * swish).astype(jnp.bfloat16)
        down_list.append(jnp.dot(active.T, rows_grad, preferred_element_type=jnp.float32).astype(jnp.bfloat16))
        gate_list.append(jnp.dot(routed.T, gate_delta, preferred_element_type=jnp.float32).astype(jnp.bfloat16))
        up_list.append(jnp.dot(routed.T, up_delta, preferred_element_type=jnp.float32).astype(jnp.bfloat16))
        routed_grad = jnp.dot(gate_delta, gate_weight[expert].T, preferred_element_type=jnp.float32)
        routed_grad = routed_grad + jnp.dot(up_delta, up_weight[expert].T, preferred_element_type=jnp.float32)
        score_grad = lax.optimization_barrier(jnp.sum(routed_grad * rows_norm.astype(jnp.float32), axis=1, keepdims=True)) * score * (1.0 - score)
        normed_grad = routed_grad * score + score_grad * column.astype(jnp.float32)[None, :]
        scaled = gain * normed_grad
        rows_out = rows_inverse * scaled - rows_hidden * rows_inverse ** 3 * lax.optimization_barrier(jnp.mean(scaled * rows_hidden, axis=1, keepdims=True))
        moe_grad = moe_grad.at[source].add(jnp.where(live, rows_out, 0.0))
    residual_grad = (out_grad.astype(jnp.float32) + moe_grad).astype(jnp.bfloat16)
    return (residual_grad, jnp.stack(gate_list), jnp.stack(up_list), jnp.stack(down_list))

def attention_part(queries, key_rows, value_rows, doc_ids, attn_grad):
    group = HQW // HKVW
    width = math.gcd(LEN, 512)
    scale = HD ** (-0.5)
    position = jnp.arange(LEN, dtype=jnp.int32)
    query_all = queries.reshape(LEN, HQW, HD)
    grad_all = attn_grad.reshape(LEN, HQW, HD)
    keys_all = key_rows.reshape(LEN, HKVW, HD)
    values_all = value_rows.reshape(LEN, HKVW, HD)
    query_parts, key_parts, value_parts = ([], [], [])
    for head in range(HKVW):
        key_one = keys_all[:, head, :].astype(jnp.float32)
        value_one = values_all[:, head, :].astype(jnp.float32)
        query_set = query_all[:, head * group:(head + 1) * group, :]
        grad_set = grad_all[:, head * group:(head + 1) * group, :]

        def block(carry, index):
            key_acc, value_acc = carry
            first = index * width
            query_blk = lax.dynamic_slice_in_dim(query_set, first, width, 0).astype(jnp.float32)
            grad_blk = lax.dynamic_slice_in_dim(grad_set, first, width, 0).astype(jnp.float32)
            query_pos = first + jnp.arange(width, dtype=jnp.int32)
            query_doc = lax.dynamic_slice_in_dim(doc_ids, first, width, 0)
            allowed = (position[None, :] <= query_pos[:, None]) & (doc_ids[None, :] == query_doc[:, None])
            allowed = allowed[None]
            logits = jnp.einsum('qgd,kd->gqk', query_blk, key_one) * scale
            top = lax.optimization_barrier(jnp.max(jnp.where(allowed, logits, NEG), axis=2, keepdims=True))
            weights = jnp.where(allowed, jnp.exp(logits - top), 0.0)
            total = lax.optimization_barrier(jnp.sum(weights, axis=2, keepdims=True))
            prob = weights / total
            prob_grad = jnp.einsum('qgd,kd->gqk', grad_blk, value_one)
            delta = lax.optimization_barrier(jnp.sum(prob * prob_grad, axis=2, keepdims=True))
            prob_half = held(prob)
            logit_grad = held(prob * (prob_grad - delta))
            query_out = jnp.einsum('gqk,kd->qgd', logit_grad, key_one) * scale
            key_acc = key_acc + jnp.einsum('gqk,qgd->kd', logit_grad, query_blk) * scale
            value_acc = value_acc + jnp.einsum('gqk,qgd->kd', prob_half, grad_blk)
            return ((key_acc, value_acc), query_out)
        zero = jnp.zeros((LEN, HD), jnp.float32)
        (key_acc, value_acc), query_out = lax.scan(block, (zero, zero), jnp.arange(LEN // width, dtype=jnp.int32))
        query_parts.append(query_out.reshape(LEN, group, HD))
        key_parts.append(key_acc)
        value_parts.append(value_acc)
    query_grad = jnp.concatenate(query_parts, axis=1).reshape(LEN, HQW * HD).astype(jnp.bfloat16)
    key_grad = jnp.stack(key_parts, axis=1).reshape(LEN, HKVW * HD).astype(jnp.bfloat16)
    value_grad = jnp.stack(value_parts, axis=1).reshape(LEN, HKVW * HD).astype(jnp.bfloat16)
    return (query_grad, key_grad, value_grad)

def reference(residual, out_grad, queries, key_rows, value_rows, doc_ids, expert_ids, norm_gain, router_columns, gate_weight, up_weight, down_weight, out_weight):
    residual_grad, grad_gate, grad_up, grad_down = expert_part(residual, out_grad, expert_ids, norm_gain, router_columns, gate_weight, up_weight, down_weight)
    attn_grad = jnp.dot(residual_grad, out_weight.T, preferred_element_type=jnp.float32).astype(jnp.bfloat16)
    query_grad, key_grad, value_grad = attention_part(queries, key_rows, value_rows, doc_ids, attn_grad)
    return (residual_grad, query_grad, key_grad, value_grad, grad_gate, grad_up, grad_down)
```

```python
import functools

import jax
import jax.numpy as jnp
from jax import lax
from jax.experimental import pallas as pl
from jax.experimental.pallas import tpu as pltpu
from jax.sharding import PartitionSpec as P

HD = 128
CAPL = 4
EPS = 1e-05
NEG = -1e30
LOG2E = 1.4426950408889634
MESH = pl.DeviceIdType.MESH
NY, NZ, NX = 4, 4, 2
CTX = NY * NZ * NX
TP = 4


def contract(left, right, left_dim, right_dim):
    return lax.dot_general(
        left, right, (((left_dim,), (right_dim,)), ((), ())), preferred_element_type=jnp.float32
    )


def place_of():
    me = lax.axis_index("ctx")
    return me // (NZ * NX), (me // NX) % NZ, me % NX


def at(y, z, x):
    return {"ctx": y * (NZ * NX) + z * NX + x}


def signal(device):
    pl.semaphore_signal(
        pltpu.get_barrier_semaphore(), inc=1, device_id=device, device_id_type=MESH
    )


def remote(src, dst, send, recv, device):
    return pltpu.make_async_remote_copy(
        src_ref=src, dst_ref=dst, send_sem=send, recv_sem=recv, device_id=device, device_id_type=MESH
    )


class Gather:
    def __init__(self, src, buf, order, send, recv, local):
        self.src, self.buf, self.order = src, buf, order
        self.send, self.recv, self.local = send, recv, local

    def copy(self, src, dst, k, device):
        return remote(src, dst, self.send.at[k], self.recv.at[k], device)

    def along_z(self, step):
        return (self.order == 0) == (step in (2, 3))

    def slab(self, step, offset, half):
        y, z, x = place_of()
        buf = self.buf
        if self.along_z(step):
            z = (z + offset) % NZ
        else:
            y = (y + offset) % NY
        if step in (2, 3):
            return buf.at[y, z] if half is None else buf.at[y, z, half]
        if self.along_z(step):
            return buf.at[:, z] if half is None else buf.at[2 * half : 2 * half + 2, z]
        return buf.at[y] if half is None else buf.at[y, 2 * half : 2 * half + 2]

    def device(self, step, offset):
        y, z, x = place_of()
        if self.along_z(step):
            return at(y, (z + offset) % NZ, x)
        return at((y + offset) % NY, z, x)

    def sends(self, step):
        y, z, x = place_of()
        if step == 1:
            return [self.copy(self.src, self.buf.at[y, z, x], 0, at(y, z, 1 - x))]
        copies = []
        for i, d in enumerate((1, 3)):
            k = 1 + 2 * (step - 2) + i
            part = self.slab(step, 0, None) if step in (2, 4) else self.slab(step, 4 - d, i)
            copies.append(self.copy(part, part, k, self.device(step, d)))
        return copies

    def receives(self, step):
        y, z, x = place_of()
        if step == 1:
            part = self.buf.at[y, z, 1 - x]
            return [self.copy(part, part, 0, at(y, z, 1 - x))]
        copies = []
        for i, d in enumerate((1, 3)):
            k = 1 + 2 * (step - 2) + i
            part = self.slab(step, 4 - d, None) if step in (2, 4) else self.slab(step, 2, i)
            copies.append(self.copy(part, part, k, self.device(step, d)))
        return copies

    def own(self):
        y, z, x = place_of()
        return pltpu.make_async_copy(self.src, self.buf.at[y, z, x], self.local)

    def start(self, step):
        if step == 1:
            self.own().start()
        for copy in self.sends(step):
            copy.start()

    def arrive(self, step):
        if step == 1:
            self.own().wait()
        for copy in self.receives(step):
            copy.wait_recv()

    def finish(self):
        for step in range(1, 6):
            for copy in self.sends(step):
                copy.wait_send()


def gather_kernel(orders, *refs):
    n = len(orders)
    ins, outs, (send, recv, local) = refs[:n], refs[n : 2 * n], refs[2 * n :]
    y, z, x = place_of()
    signal(at(y, z, 1 - x))
    for d in (1, 3):
        signal(at(y, (z + d) % NZ, x))
        signal(at((y + d) % NY, z, x))
    pl.semaphore_wait(pltpu.get_barrier_semaphore(), 5)
    parts = [
        Gather(ins[i], outs[i], orders[i], send.at[i], recv.at[i], local.at[i]) for i in range(n)
    ]
    for part in parts:
        part.start(1)
    for step in range(2, 6):
        for part in parts:
            part.arrive(step - 1)
            part.start(step)
    for part in parts:
        part.arrive(5)
    for part in parts:
        part.finish()


def gather(arrays, orders, collective_id):
    n = len(arrays)
    return pl.pallas_call(
        functools.partial(gather_kernel, orders),
        out_shape=[jax.ShapeDtypeStruct((NY, NZ, NX) + a.shape, a.dtype) for a in arrays],
        in_specs=[pl.BlockSpec(memory_space=pltpu.VMEM)] * n,
        out_specs=[pl.BlockSpec(memory_space=pltpu.VMEM)] * n,
        scratch_shapes=[
            pltpu.SemaphoreType.DMA((n, 9)),
            pltpu.SemaphoreType.DMA((n, 9)),
            pltpu.SemaphoreType.DMA((n,)),
        ],
        compiler_params=pltpu.CompilerParams(
            collective_id=collective_id, has_side_effects=True, vmem_limit_bytes=50 << 20
        ),
    )(*arrays)


def fold_rows(column):
    row = lax.broadcasted_iota(jnp.int32, (16, 16), 0) % CAPL
    col = lax.broadcasted_iota(jnp.int32, (16, 16), 1) % CAPL
    same = (row == col).astype(jnp.float32)
    wide = jnp.broadcast_to(column, (16, 128))
    return jnp.dot(
        same, wide, precision=lax.Precision.HIGHEST, preferred_element_type=jnp.float32
    )[:, :1]


def rows_kernel(
    part, normed, hidden, gain, column, score, inverse, out, slots, send, recv, tsend, trecv, local
):
    me = lax.axis_index("ctx")
    tp = lax.axis_index("tp")

    def greet(d, _):
        signal({"ctx": (me + d) % CTX})
        return 0

    lax.fori_loop(1, CTX, greet, 0)
    for d in range(1, TP):
        signal({"tp": (tp + d) % TP})
    pl.semaphore_wait(pltpu.get_barrier_semaphore(), CTX - 1 + TP - 1)

    def launch(d, _):
        to = (me + d) % CTX
        remote(part.at[to], slots.at[me], send.at[d], recv.at[d], {"ctx": to}).start()
        return 0

    lax.fori_loop(1, CTX, launch, 0)

    def collect(d, total):
        source = (me + CTX - d) % CTX
        remote(part.at[me], slots.at[source], send.at[d], recv.at[d], {"ctx": source}).wait_recv()
        return total + slots[source].astype(jnp.float32)

    routed_grad = lax.fori_loop(1, CTX, collect, part[me].astype(jnp.float32))
    normed_v = normed[...].astype(jnp.float32)
    hidden_v = hidden[...].astype(jnp.float32)
    score_v = score[:, :1]
    inverse_v = inverse[:, :1]
    dots = fold_rows(jnp.sum(routed_grad * normed_v, axis=1, keepdims=True))
    score_grad = dots * score_v * (1.0 - score_v)
    scaled = gain[...] * (routed_grad * score_v + score_grad * column[...])
    mean = fold_rows(jnp.sum(scaled * hidden_v, axis=1, keepdims=True)) * (1.0 / (4 * 1280))
    rows = inverse_v * scaled - hidden_v * (inverse_v * inverse_v * inverse_v) * mean
    out[tp] = rows.astype(jnp.bfloat16)
    for d in range(1, TP):
        remote(
            out.at[tp], out.at[tp], tsend.at[d], trecv.at[d], {"tp": (tp + d) % TP}
        ).start()
    for d in range(1, TP):
        source = (tp + TP - d) % TP
        remote(
            out.at[source], out.at[source], tsend.at[d], trecv.at[d], {"tp": source}
        ).wait_recv()
    for d in range(1, TP):
        remote(
            out.at[tp], out.at[tp], tsend.at[d], trecv.at[d], {"tp": (tp + d) % TP}
        ).wait_send()

    def drain(d, _):
        to = (me + d) % CTX
        remote(part.at[to], slots.at[me], send.at[d], recv.at[d], {"ctx": to}).wait_send()
        return 0

    lax.fori_loop(1, CTX, drain, 0)


def expert_rows(part, normed, hidden, gain, column, score, inverse, collective_id):
    return pl.pallas_call(
        rows_kernel,
        out_shape=jax.ShapeDtypeStruct((TP, 16, 1280), jnp.bfloat16),
        in_specs=[pl.BlockSpec(memory_space=pltpu.VMEM)] * 7,
        out_specs=pl.BlockSpec(memory_space=pltpu.VMEM),
        scratch_shapes=[
            pltpu.VMEM((CTX, 16, 1280), jnp.bfloat16),
            pltpu.SemaphoreType.DMA((CTX,)),
            pltpu.SemaphoreType.DMA((CTX,)),
            pltpu.SemaphoreType.DMA((TP,)),
            pltpu.SemaphoreType.DMA((TP,)),
            pltpu.SemaphoreType.DMA,
        ],
        compiler_params=pltpu.CompilerParams(
            collective_id=collective_id, has_side_effects=True, vmem_limit_bytes=50 << 20
        ),
    )(part, normed, hidden, gain, column, score, inverse)


def attention_kernel(
    heads, q, g, kx, v, low, dq, dk, dv, qt, gt, ot, dqt, stat, sent, slots, send, recv
):
    me = lax.axis_index("ctx")
    length = q.shape[0]
    factor = HD**-0.5 * LOG2E

    def greet(d, _):
        signal({"ctx": (me + d) % CTX})
        return 0

    lax.fori_loop(1, CTX, greet, 0)
    pl.semaphore_wait(pltpu.get_barrier_semaphore(), CTX - 1)

    for h in range(heads):
        cols = slice(h * HD, (h + 1) * HD)
        qt[cols, :] = q[:, cols].T
        gt[cols, :] = g[:, cols].T
    key_id = lax.broadcasted_iota(jnp.int32, (length, length), 0)
    query_id = lax.broadcasted_iota(jnp.int32, (length, length), 1)
    low_v = low[0:1, :]

    def keep(j, diagonal):
        allowed = key_id >= low_v - j * length
        return allowed & (key_id <= query_id) if diagonal else allowed

    def forward(j, diagonal):
        key = kx[j, :length, :]
        value_t = v[j].T
        allowed = keep(j, diagonal)
        for h in range(heads):
            cols = slice(h * HD, (h + 1) * HD)
            logits = jnp.dot(key, qt[cols, :], preferred_element_type=jnp.float32) * factor
            logits = jnp.where(allowed, logits, NEG)
            top = jnp.max(logits, axis=0, keepdims=True)
            if diagonal:
                weights = jnp.exp2(logits - top)
                stat[h : h + 1, :] = top
                stat[8 + h : 9 + h, :] = jnp.sum(weights, axis=0, keepdims=True)
                ot[cols, :] = jnp.dot(
                    value_t, weights.astype(jnp.bfloat16), preferred_element_type=jnp.float32
                )
            else:
                old = stat[h : h + 1, :]
                top = jnp.maximum(old, top)
                weights = jnp.exp2(logits - top)
                shrink = jnp.exp2(old - top)
                stat[h : h + 1, :] = top
                stat[8 + h : 9 + h, :] = stat[8 + h : 9 + h, :] * shrink + jnp.sum(
                    weights, axis=0, keepdims=True
                )
                ot[cols, :] = ot[cols, :] * shrink + jnp.dot(
                    value_t, weights.astype(jnp.bfloat16), preferred_element_type=jnp.float32
                )

    forward(me, True)

    def forward_step(i, _):
        forward(me - i, False)
        return 0

    lax.fori_loop(1, me + 1, forward_step, 0)
    for h in range(heads):
        cols = slice(h * HD, (h + 1) * HD)
        total = stat[8 + h : 9 + h, :]
        delta = jnp.sum(ot[cols, :] * gt[cols, :].astype(jnp.float32), axis=0, keepdims=True)
        stat[16 + h : 17 + h, :] = delta / total
        stat[h : h + 1, :] = stat[h : h + 1, :] + jnp.log2(total)

    def backward(j, diagonal):
        key = kx[j, :length, :]
        key_t = key.T
        value = v[j]
        allowed = keep(j, diagonal)
        key_sum = jnp.zeros((length, HD), jnp.float32)
        value_sum = jnp.zeros((length, HD), jnp.float32)
        for h in range(heads):
            cols = slice(h * HD, (h + 1) * HD)
            logits = jnp.dot(key, qt[cols, :], preferred_element_type=jnp.float32) * factor
            logits = jnp.where(allowed, logits, NEG)
            prob = jnp.exp2(logits - stat[h : h + 1, :])
            prob_grad = jnp.dot(value, gt[cols, :], preferred_element_type=jnp.float32)
            logit_grad = (prob * (prob_grad - stat[16 + h : 17 + h, :])).astype(jnp.bfloat16)
            value_sum += jnp.dot(
                prob.astype(jnp.bfloat16), g[:, cols], preferred_element_type=jnp.float32
            )
            key_sum += jnp.dot(logit_grad, q[:, cols], preferred_element_type=jnp.float32)
            query_part = jnp.dot(key_t, logit_grad, preferred_element_type=jnp.float32)
            dqt[cols, :] = query_part if diagonal else dqt[cols, :] + query_part
        return key_sum, value_sum

    key_own, value_own = backward(me, True)
    dk[...] = key_own.astype(jnp.bfloat16)
    dv[...] = value_own.astype(jnp.bfloat16)
    sent[me, :length, :] = key_own.astype(jnp.bfloat16)
    sent[me, length:, :] = value_own.astype(jnp.bfloat16)

    def outgoing(j):
        return remote(sent.at[j], slots.at[me], send.at[j], recv.at[me], {"ctx": j})

    def backward_step(i, _):
        j = me - i
        key_part, value_part = backward(j, False)
        sent[j, :length, :] = key_part.astype(jnp.bfloat16)
        sent[j, length:, :] = value_part.astype(jnp.bfloat16)
        outgoing(j).start()
        return 0

    lax.fori_loop(1, me + 1, backward_step, 0)
    for h in range(heads):
        cols = slice(h * HD, (h + 1) * HD)
        dq[:, cols] = (dqt[cols, :].T * HD**-0.5).astype(jnp.bfloat16)

    def collect(j, total):
        remote(sent.at[me], slots.at[j], send.at[j], recv.at[j], {"ctx": j}).wait_recv()
        return total + slots[j].astype(jnp.float32)

    total = lax.fori_loop(me + 1, CTX, collect, sent[me].astype(jnp.float32))
    dk[...] = (total[:length] * HD**-0.5).astype(jnp.bfloat16)
    dv[...] = total[length:].astype(jnp.bfloat16)

    def drain(j, _):
        outgoing(j).wait_send()
        return 0

    lax.fori_loop(0, me, drain, 0)


def attention(q, g, kx, v, low, collective_id):
    length, width = q.shape
    return pl.pallas_call(
        functools.partial(attention_kernel, width // HD),
        out_shape=[
            jax.ShapeDtypeStruct((length, width), jnp.bfloat16),
            jax.ShapeDtypeStruct((length, HD), jnp.bfloat16),
            jax.ShapeDtypeStruct((length, HD), jnp.bfloat16),
        ],
        in_specs=[pl.BlockSpec(memory_space=pltpu.VMEM)] * 5,
        out_specs=[pl.BlockSpec(memory_space=pltpu.VMEM)] * 3,
        scratch_shapes=[
            pltpu.VMEM((width, length), jnp.bfloat16),
            pltpu.VMEM((width, length), jnp.bfloat16),
            pltpu.VMEM((width, length), jnp.float32),
            pltpu.VMEM((width, length), jnp.float32),
            pltpu.VMEM((24, length), jnp.float32),
            pltpu.VMEM((CTX, 2 * length, HD), jnp.bfloat16),
            pltpu.VMEM((CTX, 2 * length, HD), jnp.bfloat16),
            pltpu.SemaphoreType.DMA((CTX,)),
            pltpu.SemaphoreType.DMA((CTX,)),
        ],
        compiler_params=pltpu.CompilerParams(
            collective_id=collective_id, has_side_effects=True, vmem_limit_bytes=50 << 20
        ),
    )(q, g, kx, v, low)


def quarters(rows):
    return rows.reshape(-1, CAPL, 4, 1280).transpose(0, 2, 1, 3).reshape(-1, 16, 1280)


def whole(blocks):
    return blocks.reshape(-1, 4, CAPL, 1280).transpose(0, 2, 1, 3).reshape(-1, 5120)


def local(
    residual,
    out_grad,
    queries,
    key_rows,
    value_rows,
    doc_ids,
    expert_ids,
    norm_gain,
    router_columns,
    gate_weight,
    up_weight,
    down_weight,
    out_weight,
):
    ctx_index = lax.axis_index("ctx")
    tp_index = lax.axis_index("tp")
    length = residual.shape[0]
    mine = (expert_ids[None, :] == jnp.arange(TP)[:, None]).astype(jnp.int32)
    slot = jnp.cumsum(mine, axis=1) - mine
    place = ((mine[:, None, :] > 0) & (slot[:, None, :] == jnp.arange(CAPL)[None, :, None])).astype(
        jnp.bfloat16
    )
    own_place = lax.dynamic_index_in_dim(place, tp_index, 0, keepdims=False)
    rows_hidden = jnp.dot(own_place, residual, preferred_element_type=jnp.float32).astype(jnp.bfloat16)
    rows_grad = jnp.dot(own_place, out_grad, preferred_element_type=jnp.float32).astype(jnp.bfloat16)
    counts = jnp.sum(
        (doc_ids[None, :] < jnp.arange(16)[:, None]).astype(jnp.float32), axis=1, keepdims=True
    )
    key_ext = jnp.concatenate(
        [key_rows, jnp.broadcast_to(counts, (16, HD)).astype(jnp.bfloat16)], axis=0
    )
    weight_t = out_weight.T
    hidden_b, grad_b, key_all, value_all, weight_b, weight_a = gather(
        [
            quarters(rows_hidden)[0],
            quarters(rows_grad)[0],
            key_ext,
            value_rows,
            weight_t[:, 384:],
            weight_t[:, :384],
        ],
        [0, 1, 0, 1, 0, 1],
        1,
    )
    key_all = key_all.reshape(CTX, length + 16, HD)
    value_all = value_all.reshape(CTX, length, HD)
    weight_a = weight_a.reshape(-1, 384)
    weight_b = weight_b.reshape(-1, 256)
    all_hidden = whole(hidden_b.reshape(CTX, 16, 1280))
    all_grad = whole(grad_b.reshape(CTX, 16, 1280))
    gain = norm_gain.astype(jnp.float32)
    hidden_all = all_hidden.astype(jnp.float32)
    inverse = lax.rsqrt(jnp.mean(hidden_all * hidden_all, axis=1, keepdims=True) + EPS)
    normed = (hidden_all * inverse * gain).astype(jnp.bfloat16)
    column = router_columns[:, 0]
    score = jax.nn.sigmoid(jnp.dot(normed, column, preferred_element_type=jnp.float32))[:, None]
    routed = (normed.astype(jnp.float32) * score).astype(jnp.bfloat16)
    gate_local = gate_weight[0]
    up_local = up_weight[0]
    down_local = down_weight[0]
    gate = jnp.dot(routed, gate_local, preferred_element_type=jnp.float32)
    upward = jnp.dot(routed, up_local, preferred_element_type=jnp.float32)
    sigma = jax.nn.sigmoid(gate)
    swish = gate * sigma
    active = (swish * upward).astype(jnp.bfloat16)
    active_grad = contract(all_grad, down_local, 1, 1)
    gate_delta = (active_grad * upward * sigma * (1.0 + gate * (1.0 - sigma))).astype(jnp.bfloat16)
    up_delta = (active_grad * swish).astype(jnp.bfloat16)
    grad_down = contract(active, all_grad, 0, 0).astype(jnp.bfloat16)[None]
    grad_gate = contract(routed, gate_delta, 0, 0).astype(jnp.bfloat16)[None]
    grad_up = contract(routed, up_delta, 0, 0).astype(jnp.bfloat16)[None]
    part = contract(gate_delta, gate_local, 1, 1) + contract(up_delta, up_local, 1, 1)
    first_row = ctx_index * CAPL

    def own(array):
        return lax.dynamic_slice_in_dim(array, first_row, CAPL, 0)

    def wide(vector):
        return jnp.broadcast_to(vector.reshape(4, 1, 1280), (4, CAPL, 1280)).reshape(16, 1280)

    def tall(array):
        return jnp.broadcast_to(jnp.tile(own(array), (4, 1)), (16, 128))

    rows = expert_rows(
        quarters(part.astype(jnp.bfloat16)),
        quarters(own(normed))[0],
        quarters(own(all_hidden))[0],
        wide(gain),
        wide(column.astype(jnp.float32)),
        tall(score),
        tall(inverse),
        2,
    )
    rows_all = whole(rows)
    moe_grad = contract(place.reshape(16, length), rows_all, 0, 0)
    residual_grad = (out_grad.astype(jnp.float32) + moe_grad).astype(jnp.bfloat16)
    attn_grad = jnp.concatenate(
        [
            jnp.dot(residual_grad, weight_a, preferred_element_type=jnp.float32).astype(jnp.bfloat16),
            jnp.dot(residual_grad, weight_b, preferred_element_type=jnp.float32).astype(jnp.bfloat16),
        ],
        axis=1,
    )
    starts = jnp.sum(key_all[:, length : length + 8, 0].astype(jnp.float32), axis=0)
    low = jnp.sum(
        jnp.where(doc_ids[None, :] == jnp.arange(8)[:, None], starts[:, None], 0.0), axis=0
    ).astype(jnp.int32)
    low = jnp.broadcast_to(low[None, :], (8, length))
    query_grad, key_grad, value_grad = attention(queries, attn_grad, key_all, value_all, low, 3)
    return (residual_grad, query_grad, key_grad, value_grad, grad_gate, grad_up, grad_down)


def solution(mesh):
    in_specs = (
        P("ctx", None),
        P("ctx", None),
        P("ctx", "tp"),
        P("ctx", "tp"),
        P("ctx", "tp"),
        P("ctx"),
        P("ctx"),
        P(),
        P(None, "tp"),
        P("tp", None, "ctx"),
        P("tp", None, "ctx"),
        P("tp", "ctx", None),
        P("tp", "ctx"),
    )
    out_specs = (
        P("ctx", None),
        P("ctx", "tp"),
        P("ctx", "tp"),
        P("ctx", "tp"),
        P("tp", None, "ctx"),
        P("tp", None, "ctx"),
        P("tp", "ctx", None),
    )
    return jax.shard_map(local, mesh=mesh, in_specs=in_specs, out_specs=out_specs, check_vma=False)
```

```python
import jax
import jax.numpy as jnp
from jax import lax
from jax.experimental import pallas as pl
from jax.experimental.pallas import tpu as pltpu
from jax.sharding import PartitionSpec as P

HD = 128
CAPL = 4
EPS = 1e-05
NEG = -1e30
LOG2E = 1.4426950408889634
MESH = pl.DeviceIdType.MESH
NY, NZ, NX = 4, 4, 2
CTX = NY * NZ * NX
TP = 4


def contract(left, right, left_dim, right_dim):
    return lax.dot_general(
        left, right, (((left_dim,), (right_dim,)), ((), ())), preferred_element_type=jnp.float32
    )


def place_of():
    me = lax.axis_index("ctx")
    return me // (NZ * NX), (me // NX) % NZ, me % NX


def at(y, z, x):
    return {"ctx": y * (NZ * NX) + z * NX + x}


def signal(device):
    pl.semaphore_signal(
        pltpu.get_barrier_semaphore(), inc=1, device_id=device, device_id_type=MESH
    )


def remote(src, dst, send, recv, device):
    return pltpu.make_async_remote_copy(
        src_ref=src, dst_ref=dst, send_sem=send, recv_sem=recv, device_id=device, device_id_type=MESH
    )


class Gather:
    def __init__(self, src, buf, order, send, recv, local):
        self.src, self.buf, self.order = src, buf, order
        self.send, self.recv, self.local = send, recv, local

    def copy(self, src, dst, k, device):
        return remote(src, dst, self.send.at[k], self.recv.at[k], device)

    def along_z(self, step):
        return (self.order == 0) == (step in (2, 3))

    def slab(self, step, offset, half):
        y, z, x = place_of()
        buf = self.buf
        if self.along_z(step):
            z = (z + offset) % NZ
        else:
            y = (y + offset) % NY
        if step in (2, 3):
            return buf.at[y, z] if half is None else buf.at[y, z, half]
        if self.along_z(step):
            return buf.at[:, z] if half is None else buf.at[2 * half : 2 * half + 2, z]
        return buf.at[y] if half is None else buf.at[y, 2 * half : 2 * half + 2]

    def device(self, step, offset):
        y, z, x = place_of()
        if self.along_z(step):
            return at(y, (z + offset) % NZ, x)
        return at((y + offset) % NY, z, x)

    def sends(self, step):
        y, z, x = place_of()
        if step == 1:
            return [self.copy(self.src, self.buf.at[y, z, x], 0, at(y, z, 1 - x))]
        copies = []
        for i, d in enumerate((1, 3)):
            k = 1 + 2 * (step - 2) + i
            part = self.slab(step, 0, None) if step in (2, 4) else self.slab(step, 4 - d, i)
            copies.append(self.copy(part, part, k, self.device(step, d)))
        return copies

    def receives(self, step):
        y, z, x = place_of()
        if step == 1:
            part = self.buf.at[y, z, 1 - x]
            return [self.copy(part, part, 0, at(y, z, 1 - x))]
        copies = []
        for i, d in enumerate((1, 3)):
            k = 1 + 2 * (step - 2) + i
            part = self.slab(step, 4 - d, None) if step in (2, 4) else self.slab(step, 2, i)
            copies.append(self.copy(part, part, k, self.device(step, d)))
        return copies

    def own(self):
        y, z, x = place_of()
        return pltpu.make_async_copy(self.src, self.buf.at[y, z, x], self.local)

    def start(self, step):
        if step == 1:
            self.own().start()
        for copy in self.sends(step):
            copy.start()

    def arrive(self, step):
        if step == 1:
            self.own().wait()
        for copy in self.receives(step):
            copy.wait_recv()

    def finish(self):
        for step in range(1, 6):
            for copy in self.sends(step):
                copy.wait_send()


BIG = 2.0**60


def fold_rows(column):
    row = lax.broadcasted_iota(jnp.int32, (16, 16), 0) & (CAPL - 1)
    col = lax.broadcasted_iota(jnp.int32, (16, 16), 1) & (CAPL - 1)
    same = (row == col).astype(jnp.float32)
    wide = jnp.broadcast_to(column, (16, 128))
    return jnp.dot(
        same, wide, precision=lax.Precision.HIGHEST, preferred_element_type=jnp.float32
    )[:, :1]


def dot(left, right):
    return jnp.dot(left, right, preferred_element_type=jnp.float32)


def split3(value):
    high = value.astype(jnp.bfloat16).astype(jnp.float32)
    rest = value - high
    middle = rest.astype(jnp.bfloat16).astype(jnp.float32)
    return high, middle, rest - middle


def kernel(
    hid, grd, kx, v, wb, wa, q, doc, gain, column, gain16, column16, scat,
    gate_hbm, up_hbm, down_hbm, og_hbm,
    res_out, routed_out, grads_out, gd_out, ud_out, act_out, dq, dk, dv,
    hbuf, gbuf, kbuf, vbuf, wbbuf, wabuf, gu, down, og, res, perm, perm_t, hx, grads, routed,
    gd, ud, act, stack, part, slots, rows, kxe, vxe, qx, gx, ot, top, sb, pb, lb, qs, gs, dqt,
    acc, dslots,
    gsend, grecv, glocal, send, recv, tsend, trecv, dsend, drecv, loads, stores,
):
    me = lax.axis_index("ctx")
    tp = lax.axis_index("tp")
    length = q.shape[0]
    heads = q.shape[1] // HD
    scale = HD**-0.5
    factor = scale * LOG2E
    features = down.shape[1]

    fetch_gate = pltpu.make_async_copy(gate_hbm, gu.at[:features], loads.at[0])
    fetch_up = pltpu.make_async_copy(up_hbm, gu.at[features:], loads.at[1])
    fetch_down = pltpu.make_async_copy(down_hbm, down, loads.at[2])
    fetch_og = pltpu.make_async_copy(og_hbm, og, loads.at[3])
    fetch_gate.start()
    fetch_up.start()
    fetch_down.start()
    fetch_og.start()

    def greet(d, _):
        signal({"ctx": (me + d) % CTX})
        return 0

    lax.fori_loop(1, CTX, greet, 0)
    for d in range(1, TP):
        signal({"tp": (tp + d) % TP})
    pl.semaphore_wait(pltpu.get_barrier_semaphore(), CTX - 1 + TP - 1)

    def piece(src, buf, order, i):
        return Gather(src, buf, order, gsend.at[i], grecv.at[i], glocal.at[i])

    moe = [piece(hid, hbuf, 0, 0), piece(grd, gbuf, 1, 1)]
    keys = [piece(kx, kbuf, 0, 2), piece(v, vbuf, 1, 3)]
    weights = [piece(wb, wbbuf, 0, 4), piece(wa, wabuf, 1, 5)]

    def go(parts, step):
        for part in parts:
            if step > 1:
                part.arrive(step - 1)
            if step < 6:
                part.start(step)

    go(moe, 1)
    go(keys, 1)
    go(weights, 1)
    go(moe, 2)
    go(moe, 3)

    def row_of(index):
        token = index & 127
        return (token >> 2) * 16 + (index >> 7) * 4 + (token & 3)

    a = lax.broadcasted_iota(jnp.int32, (512, 512), 0)
    b = lax.broadcasted_iota(jnp.int32, (512, 512), 1)
    perm[...] = (a == row_of(b)).astype(jnp.float32).astype(jnp.bfloat16)
    perm_t[...] = (b == row_of(a)).astype(jnp.float32).astype(jnp.bfloat16)
    for h in range(heads):
        cols = slice(h * HD, (h + 1) * HD)
        qs[h * length : (h + 1) * length, :] = q[:, cols]
        qx[h, :HD, :] = q[:, cols].T
        qx[h, HD:, :] = jnp.zeros((HD, length), jnp.bfloat16)
        gx[h, HD:, :] = jnp.zeros((HD, length), jnp.bfloat16)

    go(keys, 2)
    go(moe, 4)
    go(weights, 2)
    go(keys, 3)
    go(moe, 5)
    go(weights, 3)
    go(keys, 4)
    go(moe, 6)

    quarter = features // 4

    def unfold(t, _):
        cols = pl.ds(pl.multiple_of(t * 256, 256), 256)
        block = hbuf[:, :, :, :, cols].reshape(512, 256)
        hx[:, cols] = dot(perm_t[...], block).astype(jnp.bfloat16)
        block = gbuf[:, :, :, :, cols].reshape(512, 256)
        values = dot(perm_t[...], block).astype(jnp.bfloat16)
        for i in range(4):
            grads[:, pl.ds(pl.multiple_of(i * quarter + t * 256, 256), 256)] = values[
                i * 128 : (i + 1) * 128
            ]
        return 0

    lax.fori_loop(0, quarter // 256, unfold, 0)
    total = jnp.zeros((128, 1), jnp.float32)
    for i in range(4):
        x = hx[i * 128 : (i + 1) * 128, :].astype(jnp.float32)
        total += jnp.sum(x * x, axis=1, keepdims=True)
    inverse = lax.rsqrt(total * (1.0 / features) + EPS)
    total = jnp.zeros((128, 1), jnp.float32)
    for i in range(4):
        cols = slice(i * quarter, (i + 1) * quarter)
        x = hx[i * 128 : (i + 1) * 128, :].astype(jnp.float32)
        normed = (x * inverse * gain[:, cols]).astype(jnp.bfloat16)
        routed[:, cols] = normed
        total += jnp.sum(normed.astype(jnp.float32) * column[:, cols], axis=1, keepdims=True)
    score = jax.nn.sigmoid(total)
    for i in range(4):
        cols = slice(i * quarter, (i + 1) * quarter)
        routed[:, cols] = (routed[:, cols].astype(jnp.float32) * score).astype(jnp.bfloat16)
    go(keys, 5)
    fetch_gate.wait()
    fetch_up.wait()
    fetch_down.wait()
    gate = dot(routed[...], gu[:features, :])
    upward = dot(routed[...], gu[features:, :])
    active_grad = contract(grads[...], down[...], 1, 1)
    sigma = jax.nn.sigmoid(gate)
    swish = gate * sigma
    act[...] = (swish * upward).astype(jnp.bfloat16)
    gd[...] = (active_grad * upward * sigma * (1.0 + gate * (1.0 - sigma))).astype(jnp.bfloat16)
    ud[...] = (active_grad * swish).astype(jnp.bfloat16)

    def back(t, _):
        first = pl.multiple_of(t * 640, 640)
        values = contract(gd[...], gu[pl.ds(first, 640), :], 1, 1)
        values += contract(ud[...], gu[pl.ds(features + first, 640), :], 1, 1)
        line = pl.multiple_of((t // 2) * 128, 128)
        stack[pl.ds(line, 128), pl.ds(pl.multiple_of((t % 2) * 640, 640), 640)] = values.astype(
            jnp.bfloat16
        )
        return 0

    lax.fori_loop(0, 8, back, 0)

    def fold(t, _):
        cols = pl.ds(pl.multiple_of(t * 256, 256), 256)
        part[:, :, cols] = dot(perm[...], stack[:, cols]).astype(jnp.bfloat16).reshape(CTX, 16, 256)
        return 0

    lax.fori_loop(0, quarter // 256, fold, 0)

    def partial(d):
        to = (me + d) % CTX
        return remote(part.at[to], slots.at[me], send.at[d], recv.at[d], {"ctx": to})

    def launch(d, _):
        partial(d).start()
        return 0

    lax.fori_loop(1, CTX, launch, 0)
    saves = [
        pltpu.make_async_copy(src, dst, stores.at[i])
        for i, (src, dst) in enumerate(
            [(routed, routed_out), (grads, grads_out), (gd, gd_out), (ud, ud_out), (act, act_out)]
        )
    ]
    for save in saves:
        save.start()
    go(weights, 4)
    go(keys, 6)

    counts = jnp.sum(kbuf[:, :, :, length:, :].astype(jnp.float32), axis=(0, 1, 2))[:8]
    a = lax.broadcasted_iota(jnp.int32, (8, HD), 0)
    b = lax.broadcasted_iota(jnp.int32, (8, HD), 1)
    starts = jnp.sum(jnp.where(a == b, counts, 0.0), axis=0, keepdims=True)
    ends = jnp.sum(jnp.where(a == b + 1, counts, 0.0), axis=0, keepdims=True)
    lane = lax.broadcasted_iota(jnp.int32, (1, HD), 1)
    ends = jnp.where(lane == 7, float(CTX * length), ends)
    token = lax.broadcasted_iota(jnp.int32, (length, HD), 0).astype(jnp.float32)
    ones_at = (lane >= 8) & (lane < 11)
    ones_row = jnp.where(ones_at, 1.0, 0.0)
    ones_block = jnp.broadcast_to(ones_row, (length, HD)).astype(jnp.bfloat16)

    def extend(j, _):
        y, z, x = j // (NZ * NX), (j // NX) % NZ, j % NX
        lines = pl.ds(pl.multiple_of(j * length, length), length)
        first = (j * length).astype(jnp.float32)
        inside = (token >= starts - first) & (token < ends - first)
        kxe[lines, :HD] = kbuf[y, z, x, :length, :]
        kxe[lines, HD:] = jnp.where(inside, -BIG, ones_row).astype(jnp.bfloat16)
        vxe[lines, :HD] = vbuf[y, z, x]
        vxe[lines, HD:] = ones_block
        return 0

    lax.fori_loop(0, me + 1, extend, 0)
    row16 = lax.broadcasted_iota(jnp.int32, (16, length), 0)
    other = jnp.where((row16 < 8) & (row16 != doc[...]), 1.0, 0.0)
    for h in range(heads):
        qx[h, HD : HD + 16, :] = other.astype(jnp.bfloat16)
    key_id = lax.broadcasted_iota(jnp.int32, (length, length), 0)
    query_id = lax.broadcasted_iota(jnp.int32, (length, length), 1)
    ones16 = jnp.ones((16, length), jnp.bfloat16)

    def forward(j, diagonal):
        lines = pl.ds(pl.multiple_of(j * length, length), length)
        key = kxe[lines, :]
        value_t = jnp.concatenate([vxe[lines, :HD].T, ones16], axis=0)
        tops, shrinks = [], []
        for h in range(heads):
            logits = dot(key, qx[h])
            if diagonal:
                logits = jnp.where(key_id <= query_id, logits, -BIG)
            sb[:, h * length : (h + 1) * length] = logits
            new = jnp.max(logits, axis=0, keepdims=True)
            if not diagonal:
                old = top[h]
                new = jnp.maximum(old, new)
                shrinks.append(jnp.exp2((old - new) * factor))
            top[h] = new
            tops.append(new * factor)
        for h in range(heads):
            cols = slice(h * length, (h + 1) * length)
            pb[:, cols] = jnp.exp2(sb[:, cols] * factor - tops[h]).astype(jnp.bfloat16)
        for h in range(heads):
            more = dot(value_t, pb[:, h * length : (h + 1) * length])
            ot[h] = more if diagonal else ot[h] * shrinks[h] + more

    def forward_step(i, _):
        forward(me - i, False)
        return 0

    forward(me, True)
    half = (me + 1) // 2
    lax.fori_loop(1, half, forward_step, 0)
    go(weights, 5)
    lax.fori_loop(jnp.maximum(half, 1), me + 1, forward_step, 0)

    def collect(d, sums):
        source = (me + CTX - d) % CTX
        remote(part.at[me], slots.at[source], send.at[d], recv.at[d], {"ctx": source}).wait_recv()
        return sums + slots[source].astype(jnp.float32)

    routed_grad = lax.fori_loop(1, CTX, collect, part[me].astype(jnp.float32))
    hidden = hid[...].astype(jnp.float32)
    inverse = lax.rsqrt(
        fold_rows(jnp.sum(hidden * hidden, axis=1, keepdims=True)) * (1.0 / features) + EPS
    )
    normed = (hidden * inverse * gain16[...]).astype(jnp.bfloat16).astype(jnp.float32)
    score = jax.nn.sigmoid(fold_rows(jnp.sum(normed * column16[...], axis=1, keepdims=True)))
    dots = fold_rows(jnp.sum(routed_grad * normed, axis=1, keepdims=True))
    score_grad = dots * score * (1.0 - score)
    scaled = gain16[...] * (routed_grad * score + score_grad * column16[...])
    mean = fold_rows(jnp.sum(scaled * hidden, axis=1, keepdims=True)) * (1.0 / features)
    own_rows = inverse * scaled - hidden * (inverse * inverse * inverse) * mean
    rows[tp] = own_rows.astype(jnp.bfloat16)

    def swap(d, source):
        return remote(
            rows.at[source], rows.at[source], tsend.at[d], trecv.at[d], {"tp": (tp + d) % TP}
        )

    for d in range(1, TP):
        swap(d, tp).start()
    fetch_og.wait()
    for d in range(1, TP):
        swap(d, (tp + TP - d) % TP).wait_recv()

    for i in range(4):

        def add(t, _, i=i):
            cols = pl.ds(pl.multiple_of(t * 256, 256), 256)
            wide = pl.ds(pl.multiple_of(i * quarter + t * 256, 256), 256)
            more = dot(scat[i], rows[:, :, cols].reshape(TP * 16, 256))
            res[:, wide] = (og[:, wide].astype(jnp.float32) + more).astype(jnp.bfloat16)
            return 0

        lax.fori_loop(0, quarter // 256, add, 0)
    save_res = pltpu.make_async_copy(res, res_out, stores.at[5])
    save_res.start()

    go(weights, 6)
    acc[...] = jnp.zeros_like(acc)

    def project(i, _):
        y, z = i // 2, (i % 2) * 2
        left = res[:, pl.ds(pl.multiple_of(i * 640, 640), 640)]
        acc[:, :384] += dot(left, wabuf[y, pl.ds(z, 2)].reshape(640, 384))
        acc[:, 384:] += dot(left, wbbuf[y, pl.ds(z, 2)].reshape(640, 256))
        return 0

    lax.fori_loop(0, 8, project, 0)
    for h in range(heads):
        grad = acc[:, h * HD : (h + 1) * HD].astype(jnp.bfloat16)
        gs[h * length : (h + 1) * length, :] = grad
        grad_t = grad.T
        gx[h, :HD, :] = grad_t
        total = ot[h, HD : HD + 1, :]
        delta = jnp.sum(ot[h, :HD, :] * grad_t.astype(jnp.float32), axis=0, keepdims=True) / total
        high, middle, rest = split3(-delta)
        extra = jnp.where(row16 == 8, high, 0.0)
        extra = jnp.where(row16 == 9, middle, extra)
        extra = jnp.where(row16 == 10, rest, extra)
        gx[h, HD : HD + 16, :] = extra.astype(jnp.bfloat16)
        high, middle, rest = split3(-(top[h] + jnp.log2(total) * (1.0 / factor)))
        extra = jnp.where(row16 == 8, high, other)
        extra = jnp.where(row16 == 9, middle, extra)
        extra = jnp.where(row16 == 10, rest, extra)
        qx[h, HD : HD + 16, :] = extra.astype(jnp.bfloat16)

    def backward(j, diagonal):
        lines = pl.ds(pl.multiple_of(j * length, length), length)
        key = kxe[lines, :]
        key_t = kxe[lines, :HD].T
        value = vxe[lines, :]
        for h in range(heads):
            cols = slice(h * length, (h + 1) * length)
            logits = dot(key, qx[h])
            if diagonal:
                logits = jnp.where(key_id <= query_id, logits, -BIG)
            prob = jnp.exp2(logits * factor)
            lb[:, cols] = (prob * dot(value, gx[h])).astype(jnp.bfloat16)
            pb[:, cols] = prob.astype(jnp.bfloat16)
        value_sum = dot(pb[...], gs[...])
        key_sum = dot(lb[...], qs[...]) * scale
        for h in range(heads):
            more = dot(key_t, lb[:, h * length : (h + 1) * length])
            dqt[h] = more if diagonal else dqt[h] + more
        gu[lines, :HD] = key_sum.astype(jnp.bfloat16)
        gu[lines, HD:] = value_sum.astype(jnp.bfloat16)

    def outgoing(j):
        lines = pl.ds(pl.multiple_of(j * length, length), length)
        return remote(gu.at[lines], dslots.at[me], dsend.at[j], drecv.at[me], {"ctx": j})

    def backward_step(i, _):
        backward(me - i, False)
        outgoing(me - i).start()
        return 0

    backward(me, True)
    lax.fori_loop(1, me + 1, backward_step, 0)
    for h in range(heads):
        dq[:, h * HD : (h + 1) * HD] = (dqt[h].T * scale).astype(jnp.bfloat16)
    own = pl.ds(pl.multiple_of(me * length, length), length)

    def gather_sums(j, sums):
        remote(gu.at[own], dslots.at[j], dsend.at[j], drecv.at[j], {"ctx": j}).wait_recv()
        return sums + dslots[j].astype(jnp.float32)

    total = lax.fori_loop(me + 1, CTX, gather_sums, gu[own, :].astype(jnp.float32))
    dk[...] = total[:, :HD].astype(jnp.bfloat16)
    dv[...] = total[:, HD:].astype(jnp.bfloat16)

    def drain(j, _):
        outgoing(j).wait_send()
        return 0

    lax.fori_loop(0, me, drain, 0)

    def drain_partial(d, _):
        partial(d).wait_send()
        return 0

    lax.fori_loop(1, CTX, drain_partial, 0)
    for d in range(1, TP):
        swap(d, tp).wait_send()
    for piece_ in moe + keys + weights:
        piece_.finish()
    for save in saves:
        save.wait()
    save_res.wait()


def fused(hid, grd, kx, v, wb, wa, q, doc, gain, column, gain16, column16, scat, gate, up, down, og):
    length, width = q.shape
    heads = width // HD
    features = down.shape[1]
    rows = CTX * CAPL
    hidden = gate.shape[1]
    bf16, f32 = jnp.bfloat16, jnp.float32

    def shape(*dims):
        return jax.ShapeDtypeStruct(dims, bf16)

    vmem = pl.BlockSpec(memory_space=pltpu.VMEM)
    hbm = pl.BlockSpec(memory_space=pl.ANY)
    return pl.pallas_call(
        kernel,
        out_shape=[
            shape(length, features),
            shape(rows, features),
            shape(rows, features),
            shape(rows, hidden),
            shape(rows, hidden),
            shape(rows, hidden),
            shape(length, width),
            shape(length, HD),
            shape(length, HD),
        ],
        in_specs=[vmem] * 13 + [hbm] * 4,
        out_specs=[hbm] * 6 + [vmem] * 3,
        scratch_shapes=[
            pltpu.VMEM((NY, NZ, NX) + hid.shape, bf16),
            pltpu.VMEM((NY, NZ, NX) + grd.shape, bf16),
            pltpu.VMEM((NY, NZ, NX) + kx.shape, bf16),
            pltpu.VMEM((NY, NZ, NX) + v.shape, bf16),
            pltpu.VMEM((NY, NZ, NX) + wb.shape, bf16),
            pltpu.VMEM((NY, NZ, NX) + wa.shape, bf16),
            pltpu.VMEM((2 * features, hidden), bf16),
            pltpu.VMEM((hidden, features), bf16),
            pltpu.VMEM((length, features), bf16),
            pltpu.VMEM((length, features), bf16),
            pltpu.VMEM((512, 512), bf16),
            pltpu.VMEM((512, 512), bf16),
            pltpu.VMEM((512, features // 4), bf16),
            pltpu.VMEM((rows, features), bf16),
            pltpu.VMEM((rows, features), bf16),
            pltpu.VMEM((rows, hidden), bf16),
            pltpu.VMEM((rows, hidden), bf16),
            pltpu.VMEM((rows, hidden), bf16),
            pltpu.VMEM((512, features // 4), bf16),
            pltpu.VMEM((CTX, 16, features // 4), bf16),
            pltpu.VMEM((CTX, 16, features // 4), bf16),
            pltpu.VMEM((TP, 16, features // 4), bf16),
            pltpu.VMEM((CTX * length, 2 * HD), bf16),
            pltpu.VMEM((CTX * length, 2 * HD), bf16),
            pltpu.VMEM((heads, 2 * HD, length), bf16),
            pltpu.VMEM((heads, 2 * HD, length), bf16),
            pltpu.VMEM((heads, HD + 16, length), f32),
            pltpu.VMEM((heads, 1, length), f32),
            pltpu.VMEM((length, heads * length), f32),
            pltpu.VMEM((length, heads * length), bf16),
            pltpu.VMEM((length, heads * length), bf16),
            pltpu.VMEM((heads * length, HD), bf16),
            pltpu.VMEM((heads * length, HD), bf16),
            pltpu.VMEM((heads, HD, length), f32),
            pltpu.VMEM((length, width), f32),
            pltpu.VMEM((CTX, length, 2 * HD), bf16),
            pltpu.SemaphoreType.DMA((6, 9)),
            pltpu.SemaphoreType.DMA((6, 9)),
            pltpu.SemaphoreType.DMA((6,)),
            pltpu.SemaphoreType.DMA((CTX,)),
            pltpu.SemaphoreType.DMA((CTX,)),
            pltpu.SemaphoreType.DMA((TP,)),
            pltpu.SemaphoreType.DMA((TP,)),
            pltpu.SemaphoreType.DMA((CTX,)),
            pltpu.SemaphoreType.DMA((CTX,)),
            pltpu.SemaphoreType.DMA((4,)),
            pltpu.SemaphoreType.DMA((6,)),
        ],
        compiler_params=pltpu.CompilerParams(
            collective_id=1, has_side_effects=True, vmem_limit_bytes=60 << 20
        ),
    )(hid, grd, kx, v, wb, wa, q, doc, gain, column, gain16, column16, scat, gate, up, down, og)


def quarters(rows):
    return rows.reshape(CAPL, 4, -1).transpose(1, 0, 2).reshape(16, -1)


def local(
    residual,
    out_grad,
    queries,
    key_rows,
    value_rows,
    doc_ids,
    expert_ids,
    norm_gain,
    router_columns,
    gate_weight,
    up_weight,
    down_weight,
    out_weight,
):
    tp_index = lax.axis_index("tp")
    length = residual.shape[0]
    mine = (expert_ids[None, :] == jnp.arange(TP)[:, None]).astype(jnp.int32)
    slot = jnp.cumsum(mine, axis=1) - mine
    place = ((mine[:, None, :] > 0) & (slot[:, None, :] == jnp.arange(CAPL)[None, :, None])).astype(
        jnp.bfloat16
    )
    own_place = lax.dynamic_index_in_dim(place, tp_index, 0, keepdims=False)
    rows_hidden = dot(own_place, residual).astype(jnp.bfloat16)
    rows_grad = dot(own_place, out_grad).astype(jnp.bfloat16)
    scat = (
        place.transpose(2, 0, 1)[None, :, :, None, :]
        * jnp.eye(4, dtype=jnp.bfloat16)[:, None, None, :, None]
    ).reshape(4, length, TP * 16)
    counts = jnp.sum(
        (doc_ids[None, :] < jnp.arange(16)[:, None]).astype(jnp.float32), axis=1, keepdims=True
    )
    key_ext = jnp.concatenate(
        [key_rows, jnp.broadcast_to(counts, (16, HD)).astype(jnp.bfloat16)], axis=0
    )
    weight_t = out_weight.T
    gain = norm_gain.astype(jnp.float32)
    column = router_columns[:, 0].astype(jnp.float32)

    def wide(vector):
        return jnp.broadcast_to(vector.reshape(4, 1, -1), (4, CAPL, vector.size // 4)).reshape(16, -1)

    residual_grad, routed, grads, gate_delta, up_delta, active, query_grad, key_grad, value_grad = fused(
        quarters(rows_hidden),
        quarters(rows_grad),
        key_ext,
        value_rows,
        weight_t[:, 384:],
        weight_t[:, :384],
        queries,
        doc_ids[None, :],
        gain[None, :],
        column[None, :],
        wide(gain),
        wide(column),
        scat,
        gate_weight[0],
        up_weight[0],
        down_weight[0],
        out_grad,
    )
    grad_down = contract(active, grads, 0, 0).astype(jnp.bfloat16)[None]
    grad_gate = contract(routed, gate_delta, 0, 0).astype(jnp.bfloat16)[None]
    grad_up = contract(routed, up_delta, 0, 0).astype(jnp.bfloat16)[None]
    return (residual_grad, query_grad, key_grad, value_grad, grad_gate, grad_up, grad_down)


def solution(mesh):
    in_specs = (
        P("ctx", None),
        P("ctx", None),
        P("ctx", "tp"),
        P("ctx", "tp"),
        P("ctx", "tp"),
        P("ctx"),
        P("ctx"),
        P(),
        P(None, "tp"),
        P("tp", None, "ctx"),
        P("tp", None, "ctx"),
        P("tp", "ctx", None),
        P("tp", "ctx"),
    )
    out_specs = (
        P("ctx", None),
        P("ctx", "tp"),
        P("ctx", "tp"),
        P("ctx", "tp"),
        P("tp", None, "ctx"),
        P("tp", None, "ctx"),
        P("tp", "ctx", None),
    )
    return jax.shard_map(local, mesh=mesh, in_specs=in_specs, out_specs=out_specs, check_vma=False)
```

```python
import jax
import jax.numpy as jnp
from jax import lax
from jax.experimental import pallas as pl
from jax.experimental.pallas import tpu as pltpu
from jax.sharding import PartitionSpec as P

HD = 128
CAPL = 4
EPS = 1e-05
NEG = -1e30
LOG2E = 1.4426950408889634
MESH = pl.DeviceIdType.MESH
NY, NZ, NX = 4, 4, 2
CTX = NY * NZ * NX
TP = 4


def contract(left, right, left_dim, right_dim):
    return lax.dot_general(
        left, right, (((left_dim,), (right_dim,)), ((), ())), preferred_element_type=jnp.float32
    )


def place_of():
    me = lax.axis_index("ctx")
    return me // (NZ * NX), (me // NX) % NZ, me % NX


def at(y, z, x):
    return {"ctx": y * (NZ * NX) + z * NX + x}


def signal(device):
    pl.semaphore_signal(
        pltpu.get_barrier_semaphore(), inc=1, device_id=device, device_id_type=MESH
    )


def remote(src, dst, send, recv, device):
    return pltpu.make_async_remote_copy(
        src_ref=src, dst_ref=dst, send_sem=send, recv_sem=recv, device_id=device, device_id_type=MESH
    )


class Gather:
    def __init__(self, src, buf, order, send, recv, local):
        self.src, self.buf, self.order = src, buf, order
        self.send, self.recv, self.local = send, recv, local

    def copy(self, src, dst, k, device):
        return remote(src, dst, self.send.at[k], self.recv.at[k], device)

    def along_z(self, step):
        return (self.order == 0) == (step in (2, 3))

    def slab(self, step, offset, half):
        y, z, x = place_of()
        buf = self.buf
        if self.along_z(step):
            z = (z + offset) % NZ
        else:
            y = (y + offset) % NY
        if step in (2, 3):
            return buf.at[y, z] if half is None else buf.at[y, z, half]
        if self.along_z(step):
            return buf.at[:, z] if half is None else buf.at[2 * half : 2 * half + 2, z]
        return buf.at[y] if half is None else buf.at[y, 2 * half : 2 * half + 2]

    def device(self, step, offset):
        y, z, x = place_of()
        if self.along_z(step):
            return at(y, (z + offset) % NZ, x)
        return at((y + offset) % NY, z, x)

    def sends(self, step):
        y, z, x = place_of()
        if step == 1:
            return [self.copy(self.src, self.buf.at[y, z, x], 0, at(y, z, 1 - x))]
        copies = []
        for i, d in enumerate((1, 3)):
            k = 1 + 2 * (step - 2) + i
            part = self.slab(step, 0, None) if step in (2, 4) else self.slab(step, 4 - d, i)
            copies.append(self.copy(part, part, k, self.device(step, d)))
        return copies

    def receives(self, step):
        y, z, x = place_of()
        if step == 1:
            part = self.buf.at[y, z, 1 - x]
            return [self.copy(part, part, 0, at(y, z, 1 - x))]
        copies = []
        for i, d in enumerate((1, 3)):
            k = 1 + 2 * (step - 2) + i
            part = self.slab(step, 4 - d, None) if step in (2, 4) else self.slab(step, 2, i)
            copies.append(self.copy(part, part, k, self.device(step, d)))
        return copies

    def own(self):
        y, z, x = place_of()
        return pltpu.make_async_copy(self.src, self.buf.at[y, z, x], self.local)

    def start(self, step):
        if step == 1:
            self.own().start()
        for copy in self.sends(step):
            copy.start()

    def arrive(self, step):
        if step == 1:
            self.own().wait()
        for copy in self.receives(step):
            copy.wait_recv()

    def finish(self):
        for step in range(1, 6):
            for copy in self.sends(step):
                copy.wait_send()


class Scatter:
    def __init__(self, p, a1, c1, a2, c2, order, send, recv):
        self.p, self.order, self.send, self.recv = p, order, send, recv
        self.far_in, self.near_in = (a1, a2), (c1, c2)

    def along_z(self, stage):
        return (self.order == 0) == (stage == 2)

    def slab(self, stage, offset, half):
        y, z, x = place_of()
        p = self.p
        if self.along_z(stage):
            z = (z + offset) % NZ
        else:
            y = (y + offset) % NY
        if stage == 2:
            return p.at[y, z] if half is None else p.at[y, z, half : half + 1]
        if self.along_z(stage):
            return p.at[:, z] if half is None else p.at[2 * half : 2 * half + 2, z]
        return p.at[y] if half is None else p.at[y, 2 * half : 2 * half + 2]

    def device(self, stage, offset):
        y, z, x = place_of()
        if self.along_z(stage):
            return at(y, (z + offset) % NZ, x)
        return at((y + offset) % NY, z, x)

    def copies(self, stage, near):
        result = []
        for i, d in enumerate((1, 3)):
            k = 4 * (stage - 1) + 2 * near + i
            if near:
                src, dst = self.slab(stage, d, None), self.near_in[stage - 1].at[i]
            else:
                src, dst = self.slab(stage, 2, i), self.far_in[stage - 1].at[i]
            result.append(remote(src, dst, self.send.at[k], self.recv.at[k], self.device(stage, d)))
        return result

    def far(self, stage):
        for copy in self.copies(stage, 0):
            copy.start()

    def near(self, stage):
        for i, (d, copy) in enumerate(zip((1, 3), self.copies(stage, 0))):
            copy.wait_recv()
            half = self.slab(stage, d, i)
            more = self.far_in[stage - 1][i].astype(jnp.float32)
            half[...] = (half[...].astype(jnp.float32) + more).astype(jnp.bfloat16)
        for copy in self.copies(stage, 1):
            copy.start()

    def own(self, stage):
        for copy in self.copies(stage, 1):
            copy.wait_recv()
        slab = self.slab(stage, 0, None)
        arrived = self.near_in[stage - 1]
        more = arrived[0].astype(jnp.float32) + arrived[1].astype(jnp.float32)
        slab[...] = (slab[...].astype(jnp.float32) + more).astype(jnp.bfloat16)

    def swap(self):
        y, z, x = place_of()
        there = self.far_in[1].at[2]
        return remote(
            self.p.at[y, z, 1 - x], there.at[0], self.send.at[8], self.recv.at[8], at(y, z, 1 - x)
        )

    def last(self):
        self.swap().start()

    def total(self):
        y, z, x = place_of()
        self.swap().wait_recv()
        return self.p[y, z, x].astype(jnp.float32) + self.far_in[1][2, 0].astype(jnp.float32)

    def finish(self):
        for stage in (1, 2):
            for near in (0, 1):
                for copy in self.copies(stage, near):
                    copy.wait_send()
        self.swap().wait_send()


BIG = 2.0**60


def fold_rows(column):
    row = lax.broadcasted_iota(jnp.int32, (16, 16), 0) & (CAPL - 1)
    col = lax.broadcasted_iota(jnp.int32, (16, 16), 1) & (CAPL - 1)
    same = (row == col).astype(jnp.float32)
    wide = jnp.broadcast_to(column, (16, 128))
    return jnp.dot(
        same, wide, precision=lax.Precision.HIGHEST, preferred_element_type=jnp.float32
    )[:, :1]


def dot(left, right):
    return jnp.dot(left, right, preferred_element_type=jnp.float32)


def split3(value):
    high = value.astype(jnp.bfloat16).astype(jnp.float32)
    rest = value - high
    middle = rest.astype(jnp.bfloat16).astype(jnp.float32)
    return high, middle, rest - middle


def kernel(
    kin, v, wt, q, doc, eid, gain, column, gate_hbm, up_hbm, down_hbm, og_hbm, residual_hbm,
    res_out, routed_out, grads_out, gd_out, ud_out, act_out, dq, dk, dv,
    hbuf, gbuf, kbuf, vbuf, wbbuf, wabuf, gu, down, og, res, perm, perm_t, hx, grads, routed,
    gd, ud, act, part, slots, rows, kxe, vxe, qx, gx, ot, top, sb, pb, lb, qs, gs, dqt,
    acc, hid, grd, kx, scat, gain16, column16, pk, pv, ak, ck, bk, ek, av, cv, bv, ev,
    gsend, grecv, glocal, send, recv, tsend, trecv, dsend, drecv, loads, stores,
):
    me = lax.axis_index("ctx")
    tp = lax.axis_index("tp")
    length = q.shape[0]
    heads = q.shape[1] // HD
    scale = HD**-0.5
    factor = scale * LOG2E
    features = down.shape[1]

    fetch_gate = pltpu.make_async_copy(gate_hbm, gu.at[:features], loads.at[0])
    fetch_up = pltpu.make_async_copy(up_hbm, gu.at[features:], loads.at[1])
    fetch_down = pltpu.make_async_copy(down_hbm, down, loads.at[2])
    fetch_og = pltpu.make_async_copy(og_hbm, og, loads.at[3])
    fetch_residual = pltpu.make_async_copy(residual_hbm, res, loads.at[4])
    fetch_residual.start()
    fetch_og.start()
    fetch_gate.start()
    fetch_up.start()
    fetch_down.start()

    def greet(d, _):
        signal({"ctx": (me + d) % CTX})
        return 0

    lax.fori_loop(1, CTX, greet, 0)
    for d in range(1, TP):
        signal({"tp": (tp + d) % TP})

    quarter = features // 4
    row16 = lax.broadcasted_iota(jnp.int32, (16, length), 0)
    a = lax.broadcasted_iota(jnp.int32, (length, length), 0)
    b = lax.broadcasted_iota(jnp.int32, (length, length), 1)
    before = (a < b).astype(jnp.float32).astype(jnp.bfloat16)

    def in_slot(expert, slot):
        named = jnp.where(eid[...] == expert, 1.0, 0.0)
        rank = dot(named.astype(jnp.bfloat16), before)
        return jnp.where(rank == slot.astype(jnp.float32), named, 0.0)

    mine = in_slot(jnp.broadcast_to(tp, (16, length)), row16 & (CAPL - 1))
    kx[:length, :] = kin[...]
    counts = jnp.sum(jnp.where(doc[...] < row16, 1.0, 0.0), axis=1, keepdims=True)
    kx[length:, :] = jnp.broadcast_to(counts, (16, HD)).astype(jnp.bfloat16)
    fetch_residual.wait()
    fetch_og.wait()
    for src, dst in ((res, hid), (og, grd)):
        picked = jnp.zeros((16, quarter), jnp.float32)
        for i in range(4):
            take = jnp.where((row16 >> 2) == i, mine, 0.0).astype(jnp.bfloat16)
            picked += dot(take, src[:, i * quarter : (i + 1) * quarter])
        dst[...] = picked.astype(jnp.bfloat16)
    pl.semaphore_wait(pltpu.get_barrier_semaphore(), CTX - 1 + TP - 1)

    def piece(src, buf, order, i):
        return Gather(src, buf, order, gsend.at[i], grecv.at[i], glocal.at[i])

    moe = [piece(hid, hbuf, 0, 0), piece(grd, gbuf, 1, 1)]
    keys = [piece(kx, kbuf, 0, 2), piece(v, vbuf, 1, 3)]
    weights = [piece(wt.at[:, 384:], wbbuf, 0, 4), piece(wt.at[:, :384], wabuf, 1, 5)]

    def go(parts, step):
        for part in parts:
            if step > 1:
                part.arrive(step - 1)
            if step < 6:
                part.start(step)

    go(moe, 1)
    go(keys, 1)
    go(weights, 1)
    go(moe, 2)
    go(moe, 3)

    def row_of(index):
        token = index & 127
        return (token >> 2) * 16 + (index >> 7) * 4 + (token & 3)

    a = lax.broadcasted_iota(jnp.int32, (512, 512), 0)
    b = lax.broadcasted_iota(jnp.int32, (512, 512), 1)
    perm[...] = (a == row_of(b)).astype(jnp.float32).astype(jnp.bfloat16)
    perm_t[...] = (b == row_of(a)).astype(jnp.float32).astype(jnp.bfloat16)
    row64 = lax.broadcasted_iota(jnp.int32, (64, length), 0)
    placed = in_slot(row64 >> 4, row64 & (CAPL - 1))
    wide16 = lax.broadcasted_iota(jnp.int32, (16, quarter), 0) >> 2
    gain16[...] = jnp.zeros_like(gain16)
    column16[...] = jnp.zeros_like(column16)
    for i in range(4):
        cols = slice(i * quarter, (i + 1) * quarter)
        gain16[...] += jnp.where(wide16 == i, gain[:, cols].astype(jnp.float32), 0.0)
        column16[...] += jnp.where(wide16 == i, column[:, cols].astype(jnp.float32), 0.0)
        scat[i] = jnp.where(((row64 >> 2) & 3) == i, placed, 0.0).T.astype(jnp.bfloat16)
    for h in range(heads):
        cols = slice(h * HD, (h + 1) * HD)
        qs[h * length : (h + 1) * length, :] = q[:, cols]
        qx[h, :HD, :] = q[:, cols].T
        qx[h, HD:, :] = jnp.zeros((HD, length), jnp.bfloat16)
        gx[h, HD:, :] = jnp.zeros((HD, length), jnp.bfloat16)

    go(keys, 2)
    go(moe, 4)
    go(weights, 2)
    go(keys, 3)
    go(moe, 5)
    go(weights, 3)
    go(keys, 4)
    go(moe, 6)


    def unfold(t, _):
        cols = pl.ds(pl.multiple_of(t * 256, 256), 256)
        block = hbuf[:, :, :, :, cols].reshape(512, 256)
        hx[:, cols] = dot(perm_t[...], block).astype(jnp.bfloat16)
        block = gbuf[:, :, :, :, cols].reshape(512, 256)
        values = dot(perm_t[...], block).astype(jnp.bfloat16)
        for i in range(4):
            grads[:, pl.ds(pl.multiple_of(i * quarter + t * 256, 256), 256)] = values[
                i * 128 : (i + 1) * 128
            ]
        return 0

    lax.fori_loop(0, quarter // 256, unfold, 0)
    total = jnp.zeros((128, 1), jnp.float32)
    for i in range(4):
        x = hx[i * 128 : (i + 1) * 128, :].astype(jnp.float32)
        total += jnp.sum(x * x, axis=1, keepdims=True)
    inverse = lax.rsqrt(total * (1.0 / features) + EPS)
    total = jnp.zeros((128, 1), jnp.float32)
    for i in range(4):
        cols = slice(i * quarter, (i + 1) * quarter)
        x = hx[i * 128 : (i + 1) * 128, :].astype(jnp.float32)
        normed = (x * inverse * gain[:, cols].astype(jnp.float32)).astype(jnp.bfloat16)
        routed[:, cols] = normed
        total += jnp.sum(normed.astype(jnp.float32) * column[:, cols].astype(jnp.float32), axis=1, keepdims=True)
    score = jax.nn.sigmoid(total)
    for i in range(4):
        cols = slice(i * quarter, (i + 1) * quarter)
        routed[:, cols] = (routed[:, cols].astype(jnp.float32) * score).astype(jnp.bfloat16)
    go(keys, 5)
    fetch_gate.wait()
    fetch_up.wait()
    fetch_down.wait()
    gate = dot(routed[...], gu[:features, :])
    upward = dot(routed[...], gu[features:, :])
    active_grad = contract(grads[...], down[...], 1, 1)
    sigma = jax.nn.sigmoid(gate)
    swish = gate * sigma
    act[...] = (swish * upward).astype(jnp.bfloat16)
    gd[...] = (active_grad * upward * sigma * (1.0 + gate * (1.0 - sigma))).astype(jnp.bfloat16)
    ud[...] = (active_grad * swish).astype(jnp.bfloat16)

    def back(t, _):
        first = pl.multiple_of(t * 640, 640)
        values = contract(gd[...], gu[pl.ds(first, 640), :], 1, 1)
        values += contract(ud[...], gu[pl.ds(features + first, 640), :], 1, 1)
        line = pl.multiple_of((t // 2) * 128, 128)
        hx[pl.ds(line, 128), pl.ds(pl.multiple_of((t % 2) * 640, 640), 640)] = values.astype(
            jnp.bfloat16
        )
        return 0

    lax.fori_loop(0, 8, back, 0)

    def fold(t, _):
        cols = pl.ds(pl.multiple_of(t * 256, 256), 256)
        part[:, :, cols] = dot(perm[...], hx[:, cols]).astype(jnp.bfloat16).reshape(CTX, 16, 256)
        return 0

    lax.fori_loop(0, quarter // 256, fold, 0)

    def partial(d):
        to = (me + d) % CTX
        return remote(part.at[to], slots.at[me], send.at[d], recv.at[d], {"ctx": to})

    def launch(d, _):
        partial(d).start()
        return 0

    lax.fori_loop(1, CTX, launch, 0)
    saves = [
        pltpu.make_async_copy(src, dst, stores.at[i])
        for i, (src, dst) in enumerate(
            [(routed, routed_out), (grads, grads_out), (gd, gd_out), (ud, ud_out), (act, act_out)]
        )
    ]
    for save in saves:
        save.start()
    go(weights, 4)
    go(keys, 6)

    counts = jnp.sum(kbuf[:, :, :, length:, :].astype(jnp.float32), axis=(0, 1, 2))[:8]
    a = lax.broadcasted_iota(jnp.int32, (8, HD), 0)
    b = lax.broadcasted_iota(jnp.int32, (8, HD), 1)
    starts = jnp.sum(jnp.where(a == b, counts, 0.0), axis=0, keepdims=True)
    ends = jnp.sum(jnp.where(a == b + 1, counts, 0.0), axis=0, keepdims=True)
    lane = lax.broadcasted_iota(jnp.int32, (1, HD), 1)
    ends = jnp.where(lane == 7, float(CTX * length), ends)
    token = lax.broadcasted_iota(jnp.int32, (length, HD), 0).astype(jnp.float32)
    ones_at = (lane >= 8) & (lane < 11)
    ones_row = jnp.where(ones_at, 1.0, 0.0)
    ones_block = jnp.broadcast_to(ones_row, (length, HD)).astype(jnp.bfloat16)

    def extend(j, _):
        y, z, x = j // (NZ * NX), (j // NX) % NZ, j % NX
        lines = pl.ds(pl.multiple_of(j * length, length), length)
        first = (j * length).astype(jnp.float32)
        inside = (token >= starts - first) & (token < ends - first)
        kxe[lines, :HD] = kbuf[y, z, x, :length, :]
        kxe[lines, HD:] = jnp.where(inside, -BIG, ones_row).astype(jnp.bfloat16)
        vxe[lines, :HD] = vbuf[y, z, x]
        vxe[lines, HD:] = ones_block
        return 0

    lax.fori_loop(0, me + 1, extend, 0)
    other = jnp.where((row16 < 8) & (row16 != doc[...]), 1.0, 0.0)
    for h in range(heads):
        qx[h, HD : HD + 16, :] = other.astype(jnp.bfloat16)
    key_id = lax.broadcasted_iota(jnp.int32, (length, length), 0)
    query_id = lax.broadcasted_iota(jnp.int32, (length, length), 1)
    ones16 = jnp.ones((16, length), jnp.bfloat16)

    def forward(j, diagonal):
        lines = pl.ds(pl.multiple_of(j * length, length), length)
        key = kxe[lines, :]
        value_t = jnp.concatenate([vxe[lines, :HD].T, ones16], axis=0)
        tops, shrinks = [], []
        for h in range(heads):
            logits = dot(key, qx[h])
            if diagonal:
                logits = jnp.where(key_id <= query_id, logits, -BIG)
            sb[:, h * length : (h + 1) * length] = logits
            new = jnp.max(logits, axis=0, keepdims=True)
            if not diagonal:
                old = top[h]
                new = jnp.maximum(old, new)
                shrinks.append(jnp.exp2((old - new) * factor))
            top[h] = new
            tops.append(new * factor)
        for h in range(heads):
            cols = slice(h * length, (h + 1) * length)
            pb[:, cols] = jnp.exp2(sb[:, cols] * factor - tops[h]).astype(jnp.bfloat16)
        for h in range(heads):
            more = dot(value_t, pb[:, h * length : (h + 1) * length])
            ot[h] = more if diagonal else ot[h] * shrinks[h] + more

    def forward_step(i, _):
        forward(me - i, False)
        return 0

    forward(me, True)
    half = (me + 1) // 2
    lax.fori_loop(1, half, forward_step, 0)
    go(weights, 5)
    lax.fori_loop(jnp.maximum(half, 1), me + 1, forward_step, 0)

    def collect(d, sums):
        source = (me + CTX - d) % CTX
        remote(part.at[me], slots.at[source], send.at[d], recv.at[d], {"ctx": source}).wait_recv()
        return sums + slots[source].astype(jnp.float32)

    routed_grad = lax.fori_loop(1, CTX, collect, part[me].astype(jnp.float32))
    hidden = hid[...].astype(jnp.float32)
    inverse = lax.rsqrt(
        fold_rows(jnp.sum(hidden * hidden, axis=1, keepdims=True)) * (1.0 / features) + EPS
    )
    normed = (hidden * inverse * gain16[...]).astype(jnp.bfloat16).astype(jnp.float32)
    score = jax.nn.sigmoid(fold_rows(jnp.sum(normed * column16[...], axis=1, keepdims=True)))
    dots = fold_rows(jnp.sum(routed_grad * normed, axis=1, keepdims=True))
    score_grad = dots * score * (1.0 - score)
    scaled = gain16[...] * (routed_grad * score + score_grad * column16[...])
    mean = fold_rows(jnp.sum(scaled * hidden, axis=1, keepdims=True)) * (1.0 / features)
    own_rows = inverse * scaled - hidden * (inverse * inverse * inverse) * mean
    rows[tp] = own_rows.astype(jnp.bfloat16)

    def swap(d, source):
        return remote(
            rows.at[source], rows.at[source], tsend.at[d], trecv.at[d], {"tp": (tp + d) % TP}
        )

    for d in range(1, TP):
        swap(d, tp).start()
    for d in range(1, TP):
        swap(d, (tp + TP - d) % TP).wait_recv()

    for i in range(4):

        def add(t, _, i=i):
            cols = pl.ds(pl.multiple_of(t * 256, 256), 256)
            wide = pl.ds(pl.multiple_of(i * quarter + t * 256, 256), 256)
            more = dot(scat[i], rows[:, :, cols].reshape(TP * 16, 256))
            res[:, wide] = (og[:, wide].astype(jnp.float32) + more).astype(jnp.bfloat16)
            return 0

        lax.fori_loop(0, quarter // 256, add, 0)
    save_res = pltpu.make_async_copy(res, res_out, stores.at[5])
    save_res.start()

    go(weights, 6)
    acc[...] = jnp.zeros_like(acc)

    def project(i, _):
        y, z = i // 2, (i % 2) * 2
        left = res[:, pl.ds(pl.multiple_of(i * 640, 640), 640)]
        acc[:, :384] += dot(left, wabuf[y, pl.ds(z, 2)].reshape(640, 384))
        acc[:, 384:] += dot(left, wbbuf[y, pl.ds(z, 2)].reshape(640, 256))
        return 0

    lax.fori_loop(0, 8, project, 0)
    for h in range(heads):
        grad = acc[:, h * HD : (h + 1) * HD].astype(jnp.bfloat16)
        gs[h * length : (h + 1) * length, :] = grad
        grad_t = grad.T
        gx[h, :HD, :] = grad_t
        total = ot[h, HD : HD + 1, :]
        delta = jnp.sum(ot[h, :HD, :] * grad_t.astype(jnp.float32), axis=0, keepdims=True) / total
        high, middle, rest = split3(-delta)
        extra = jnp.where(row16 == 8, high, 0.0)
        extra = jnp.where(row16 == 9, middle, extra)
        extra = jnp.where(row16 == 10, rest, extra)
        gx[h, HD : HD + 16, :] = extra.astype(jnp.bfloat16)
        high, middle, rest = split3(-(top[h] + jnp.log2(total) * (1.0 / factor)))
        extra = jnp.where(row16 == 8, high, other)
        extra = jnp.where(row16 == 9, middle, extra)
        extra = jnp.where(row16 == 10, rest, extra)
        qx[h, HD : HD + 16, :] = extra.astype(jnp.bfloat16)

    def backward(j, diagonal):
        lines = pl.ds(pl.multiple_of(j * length, length), length)
        key = kxe[lines, :]
        key_t = kxe[lines, :HD].T
        value = vxe[lines, :]
        for h in range(heads):
            cols = slice(h * length, (h + 1) * length)
            logits = dot(key, qx[h])
            if diagonal:
                logits = jnp.where(key_id <= query_id, logits, -BIG)
            prob = jnp.exp2(logits * factor)
            lb[:, cols] = (prob * dot(value, gx[h])).astype(jnp.bfloat16)
            pb[:, cols] = prob.astype(jnp.bfloat16)
        value_sum = dot(pb[...], gs[...])
        key_sum = dot(lb[...], qs[...]) * scale
        for h in range(heads):
            more = dot(key_t, lb[:, h * length : (h + 1) * length])
            dqt[h] = dqt[h] + more
        y, z, x = j // (NZ * NX), (j // NX) % NZ, j % NX
        pk[y, z, x] = key_sum.astype(jnp.bfloat16)
        pv[y, z, x] = value_sum.astype(jnp.bfloat16)

    sums = [
        Scatter(pk, ak, ck, bk, ek, 0, dsend.at[0], drecv.at[0]),
        Scatter(pv, av, cv, bv, ev, 1, dsend.at[1], drecv.at[1]),
    ]
    y, z, x = place_of()
    for h in range(heads):
        dqt[h] = jnp.zeros((HD, length), jnp.float32)

    def backward_step(i, _):
        r = jnp.where(i < 14, i - 8, i - 14)
        turn = jnp.where(i < 14, r // 2, r // 6)
        to_y = (y + 3 - 2 * turn + turn // 2) % NY
        turn = (r % 6) // 2
        to_z = (z + 3 - 2 * turn + turn // 2) % NZ
        to_y = jnp.where(i < 8, (y + 2) % NY, to_y)
        to_z = jnp.where(i < 8, i // 2, jnp.where(i < 14, (z + 2) % NZ, to_z))
        j = to_y * (NZ * NX) + to_z * NX + i % 2

        @pl.when(j < me)
        def _():
            backward(j, False)

        @pl.when(j == me)
        def _():
            backward(j, True)

        @pl.when(j > me)
        def _():
            pk[to_y, to_z, i % 2] = jnp.zeros((length, HD), jnp.bfloat16)
            pv[to_y, to_z, i % 2] = jnp.zeros((length, HD), jnp.bfloat16)

        @pl.when(i == 7)
        def _():
            sums[0].far(1)

        @pl.when(i == 13)
        def _():
            sums[1].far(1)

        @pl.when(i == 25)
        def _():
            sums[0].near(1)

        @pl.when(i == 29)
        def _():
            sums[1].near(1)

        return 0

    lax.fori_loop(0, CTX, backward_step, 0)
    for part_ in sums:
        part_.own(1)
        part_.far(2)
    for h in range(heads):
        dq[:, h * HD : (h + 1) * HD] = (dqt[h].T * scale).astype(jnp.bfloat16)
    for part_ in sums:
        part_.near(2)
    for part_ in sums:
        part_.own(2)
        part_.last()
    dk[...] = sums[0].total().astype(jnp.bfloat16)
    dv[...] = sums[1].total().astype(jnp.bfloat16)
    for part_ in sums:
        part_.finish()

    def drain_partial(d, _):
        partial(d).wait_send()
        return 0

    lax.fori_loop(1, CTX, drain_partial, 0)
    for d in range(1, TP):
        swap(d, tp).wait_send()
    for piece_ in moe + keys + weights:
        piece_.finish()
    for save in saves:
        save.wait()
    save_res.wait()


def fused(kin, v, wt, q, doc, eid, gain, column, gate, up, down, og, residual):
    length, width = q.shape
    heads = width // HD
    features = down.shape[1]
    rows = CTX * CAPL
    hidden = gate.shape[1]
    bf16, f32 = jnp.bfloat16, jnp.float32

    def shape(*dims):
        return jax.ShapeDtypeStruct(dims, bf16)

    vmem = pl.BlockSpec(memory_space=pltpu.VMEM)
    hbm = pl.BlockSpec(memory_space=pl.ANY)
    return pl.pallas_call(
        kernel,
        out_shape=[
            shape(length, features),
            shape(rows, features),
            shape(rows, features),
            shape(rows, hidden),
            shape(rows, hidden),
            shape(rows, hidden),
            shape(length, width),
            shape(length, HD),
            shape(length, HD),
        ],
        in_specs=[vmem] * 8 + [hbm] * 5,
        out_specs=[hbm] * 6 + [vmem] * 3,
        scratch_shapes=[
            pltpu.VMEM((NY, NZ, NX) + (16, features // 4), bf16),
            pltpu.VMEM((NY, NZ, NX) + (16, features // 4), bf16),
            pltpu.VMEM((NY, NZ, NX) + (length + 16, HD), bf16),
            pltpu.VMEM((NY, NZ, NX) + v.shape, bf16),
            pltpu.VMEM((NY, NZ, NX) + (wt.shape[0], 256), bf16),
            pltpu.VMEM((NY, NZ, NX) + (wt.shape[0], 384), bf16),
            pltpu.VMEM((2 * features, hidden), bf16),
            pltpu.VMEM((hidden, features), bf16),
            pltpu.VMEM((length, features), bf16),
            pltpu.VMEM((length, features), bf16),
            pltpu.VMEM((512, 512), bf16),
            pltpu.VMEM((512, 512), bf16),
            pltpu.VMEM((512, features // 4), bf16),
            pltpu.VMEM((rows, features), bf16),
            pltpu.VMEM((rows, features), bf16),
            pltpu.VMEM((rows, hidden), bf16),
            pltpu.VMEM((rows, hidden), bf16),
            pltpu.VMEM((rows, hidden), bf16),
            pltpu.VMEM((CTX, 16, features // 4), bf16),
            pltpu.VMEM((CTX, 16, features // 4), bf16),
            pltpu.VMEM((TP, 16, features // 4), bf16),
            pltpu.VMEM((CTX * length, 2 * HD), bf16),
            pltpu.VMEM((CTX * length, 2 * HD), bf16),
            pltpu.VMEM((heads, 2 * HD, length), bf16),
            pltpu.VMEM((heads, 2 * HD, length), bf16),
            pltpu.VMEM((heads, HD + 16, length), f32),
            pltpu.VMEM((heads, 1, length), f32),
            pltpu.VMEM((length, heads * length), f32),
            pltpu.VMEM((length, heads * length), bf16),
            pltpu.VMEM((length, heads * length), bf16),
            pltpu.VMEM((heads * length, HD), bf16),
            pltpu.VMEM((heads * length, HD), bf16),
            pltpu.VMEM((heads, HD, length), f32),
            pltpu.VMEM((length, width), f32),
            pltpu.VMEM((16, features // 4), bf16),
            pltpu.VMEM((16, features // 4), bf16),
            pltpu.VMEM((length + 16, HD), bf16),
            pltpu.VMEM((4, length, 64), bf16),
            pltpu.VMEM((16, features // 4), f32),
            pltpu.VMEM((16, features // 4), f32),
            pltpu.VMEM((NY, NZ, NX, length, HD), bf16),
            pltpu.VMEM((NY, NZ, NX, length, HD), bf16),
            pltpu.VMEM((2, 2, 2, length, HD), bf16),
            pltpu.VMEM((2, 4, 2, length, HD), bf16),
            pltpu.VMEM((3, 1, length, HD), bf16),
            pltpu.VMEM((2, 2, length, HD), bf16),
            pltpu.VMEM((2, 2, 2, length, HD), bf16),
            pltpu.VMEM((2, 4, 2, length, HD), bf16),
            pltpu.VMEM((3, 1, length, HD), bf16),
            pltpu.VMEM((2, 2, length, HD), bf16),
            pltpu.SemaphoreType.DMA((6, 9)),
            pltpu.SemaphoreType.DMA((6, 9)),
            pltpu.SemaphoreType.DMA((6,)),
            pltpu.SemaphoreType.DMA((CTX,)),
            pltpu.SemaphoreType.DMA((CTX,)),
            pltpu.SemaphoreType.DMA((TP,)),
            pltpu.SemaphoreType.DMA((TP,)),
            pltpu.SemaphoreType.DMA((2, 9)),
            pltpu.SemaphoreType.DMA((2, 9)),
            pltpu.SemaphoreType.DMA((5,)),
            pltpu.SemaphoreType.DMA((6,)),
        ],
        compiler_params=pltpu.CompilerParams(
            collective_id=1, has_side_effects=True, vmem_limit_bytes=60 << 20
        ),
    )(kin, v, wt, q, doc, eid, gain, column, gate, up, down, og, residual)


def products_kernel(routed, grads, gd, ud, act, gate, up, down):
    gate[...] = contract(routed[...], gd[...], 0, 0).astype(jnp.bfloat16)
    up[...] = contract(routed[...], ud[...], 0, 0).astype(jnp.bfloat16)
    down[...] = contract(act[...], grads[...], 0, 0).astype(jnp.bfloat16)


def products(routed, grads, gd, ud, act):
    rows, features = routed.shape
    hidden = gd.shape[1]
    width = 512
    tall = pl.BlockSpec((width, hidden), lambda i: (i, 0))
    wide = pl.BlockSpec((rows, width), lambda i: (0, i))
    fixed = pl.BlockSpec((rows, hidden), lambda i: (0, 0))
    return pl.pallas_call(
        products_kernel,
        grid=(features // width,),
        out_shape=[
            jax.ShapeDtypeStruct((features, hidden), jnp.bfloat16),
            jax.ShapeDtypeStruct((features, hidden), jnp.bfloat16),
            jax.ShapeDtypeStruct((hidden, features), jnp.bfloat16),
        ],
        in_specs=[wide, wide, fixed, fixed, fixed],
        out_specs=[tall, tall, pl.BlockSpec((hidden, width), lambda i: (0, i))],
    )(routed, grads, gd, ud, act)


def local(
    residual,
    out_grad,
    queries,
    key_rows,
    value_rows,
    doc_ids,
    expert_ids,
    norm_gain,
    router_columns,
    gate_weight,
    up_weight,
    down_weight,
    out_weight,
):
    residual_grad, routed, grads, gate_delta, up_delta, active, query_grad, key_grad, value_grad = fused(
        key_rows,
        value_rows,
        out_weight.T,
        queries,
        doc_ids[None, :],
        expert_ids[None, :],
        norm_gain[None, :],
        router_columns.reshape(1, -1),
        gate_weight[0],
        up_weight[0],
        down_weight[0],
        out_grad,
        residual,
    )
    grad_gate, grad_up, grad_down = products(routed, grads, gate_delta, up_delta, active)
    return (
        residual_grad, query_grad, key_grad, value_grad, grad_gate[None], grad_up[None], grad_down[None]
    )


def solution(mesh):
    in_specs = (
        P("ctx", None),
        P("ctx", None),
        P("ctx", "tp"),
        P("ctx", "tp"),
        P("ctx", "tp"),
        P("ctx"),
        P("ctx"),
        P(),
        P(None, "tp"),
        P("tp", None, "ctx"),
        P("tp", None, "ctx"),
        P("tp", "ctx", None),
        P("tp", "ctx"),
    )
    out_specs = (
        P("ctx", None),
        P("ctx", "tp"),
        P("ctx", "tp"),
        P("ctx", "tp"),
        P("tp", None, "ctx"),
        P("tp", None, "ctx"),
        P("tp", "ctx", None),
    )
    return jax.shard_map(local, mesh=mesh, in_specs=in_specs, out_specs=out_specs, check_vma=False)
```

```python
import jax
import jax.numpy as jnp
from jax import lax
from jax.experimental import pallas as pl
from jax.experimental.pallas import tpu as pltpu
from jax.sharding import PartitionSpec as P

HD = 128
CAPL = 4
EPS = 1e-05
NEG = -1e30
LOG2E = 1.4426950408889634
MESH = pl.DeviceIdType.MESH
NY, NZ, NX = 4, 4, 2
CTX = NY * NZ * NX
TP = 4


def contract(left, right, left_dim, right_dim):
    return lax.dot_general(
        left, right, (((left_dim,), (right_dim,)), ((), ())), preferred_element_type=jnp.float32
    )


def place_of():
    me = lax.axis_index("ctx")
    return me // (NZ * NX), (me // NX) % NZ, me % NX


def at(y, z, x):
    return {"ctx": y * (NZ * NX) + z * NX + x}


def signal(device):
    pl.semaphore_signal(
        pltpu.get_barrier_semaphore(), inc=1, device_id=device, device_id_type=MESH
    )


def remote(src, dst, send, recv, device):
    return pltpu.make_async_remote_copy(
        src_ref=src, dst_ref=dst, send_sem=send, recv_sem=recv, device_id=device, device_id_type=MESH
    )


class Gather:
    def __init__(self, src, buf, order, send, recv, local):
        self.src, self.buf, self.order = src, buf, order
        self.send, self.recv, self.local = send, recv, local

    def copy(self, src, dst, k, device):
        return remote(src, dst, self.send.at[k], self.recv.at[k], device)

    def along_z(self, step):
        return (self.order == 0) == (step in (2, 3))

    def slab(self, step, offset, half):
        y, z, x = place_of()
        buf = self.buf
        if self.along_z(step):
            z = (z + offset) % NZ
        else:
            y = (y + offset) % NY
        if step in (2, 3):
            return buf.at[y, z] if half is None else buf.at[y, z, half]
        if self.along_z(step):
            return buf.at[:, z] if half is None else buf.at[2 * half : 2 * half + 2, z]
        return buf.at[y] if half is None else buf.at[y, 2 * half : 2 * half + 2]

    def device(self, step, offset):
        y, z, x = place_of()
        if self.along_z(step):
            return at(y, (z + offset) % NZ, x)
        return at((y + offset) % NY, z, x)

    def sends(self, step):
        y, z, x = place_of()
        if step == 1:
            return [self.copy(self.src, self.buf.at[y, z, x], 0, at(y, z, 1 - x))]
        copies = []
        for i, d in enumerate((1, 3)):
            k = 1 + 2 * (step - 2) + i
            part = self.slab(step, 0, None) if step in (2, 4) else self.slab(step, 4 - d, i)
            copies.append(self.copy(part, part, k, self.device(step, d)))
        return copies

    def receives(self, step):
        y, z, x = place_of()
        if step == 1:
            part = self.buf.at[y, z, 1 - x]
            return [self.copy(part, part, 0, at(y, z, 1 - x))]
        copies = []
        for i, d in enumerate((1, 3)):
            k = 1 + 2 * (step - 2) + i
            part = self.slab(step, 4 - d, None) if step in (2, 4) else self.slab(step, 2, i)
            copies.append(self.copy(part, part, k, self.device(step, d)))
        return copies

    def own(self):
        y, z, x = place_of()
        return pltpu.make_async_copy(self.src, self.buf.at[y, z, x], self.local)

    def start(self, step):
        if step == 1:
            self.own().start()
        for copy in self.sends(step):
            copy.start()

    def arrive(self, step):
        if step == 1:
            self.own().wait()
        for copy in self.receives(step):
            copy.wait_recv()

    def finish(self):
        for step in range(1, 6):
            for copy in self.sends(step):
                copy.wait_send()


class Scatter:
    def __init__(self, p, a1, c1, a2, c2, order, send, recv):
        self.p, self.order, self.send, self.recv = p, order, send, recv
        self.far_in, self.near_in = (a1, a2), (c1, c2)

    def along_z(self, stage):
        return (self.order == 0) == (stage == 2)

    def slab(self, stage, offset, half):
        y, z, x = place_of()
        p = self.p
        if self.along_z(stage):
            z = (z + offset) % NZ
        else:
            y = (y + offset) % NY
        if stage == 2:
            return p.at[y, z] if half is None else p.at[y, z, half : half + 1]
        if self.along_z(stage):
            return p.at[:, z] if half is None else p.at[2 * half : 2 * half + 2, z]
        return p.at[y] if half is None else p.at[y, 2 * half : 2 * half + 2]

    def device(self, stage, offset):
        y, z, x = place_of()
        if self.along_z(stage):
            return at(y, (z + offset) % NZ, x)
        return at((y + offset) % NY, z, x)

    def copies(self, stage, near):
        result = []
        for i, d in enumerate((1, 3)):
            k = 4 * (stage - 1) + 2 * near + i
            if near:
                src, dst = self.slab(stage, d, None), self.near_in[stage - 1].at[i]
            else:
                src, dst = self.slab(stage, 2, i), self.far_in[stage - 1].at[i]
            result.append(remote(src, dst, self.send.at[k], self.recv.at[k], self.device(stage, d)))
        return result

    def far(self, stage):
        for copy in self.copies(stage, 0):
            copy.start()

    def near(self, stage):
        for i, (d, copy) in enumerate(zip((1, 3), self.copies(stage, 0))):
            copy.wait_recv()
            half = self.slab(stage, d, i)
            more = self.far_in[stage - 1][i].astype(jnp.float32)
            half[...] = (half[...].astype(jnp.float32) + more).astype(jnp.bfloat16)
        for copy in self.copies(stage, 1):
            copy.start()

    def own(self, stage):
        for copy in self.copies(stage, 1):
            copy.wait_recv()
        slab = self.slab(stage, 0, None)
        arrived = self.near_in[stage - 1]
        more = arrived[0].astype(jnp.float32) + arrived[1].astype(jnp.float32)
        slab[...] = (slab[...].astype(jnp.float32) + more).astype(jnp.bfloat16)

    def swap(self):
        y, z, x = place_of()
        there = self.far_in[1].at[2]
        return remote(
            self.p.at[y, z, 1 - x], there.at[0], self.send.at[8], self.recv.at[8], at(y, z, 1 - x)
        )

    def last(self):
        self.swap().start()

    def total(self):
        y, z, x = place_of()
        self.swap().wait_recv()
        return self.p[y, z, x].astype(jnp.float32) + self.far_in[1][2, 0].astype(jnp.float32)

    def finish(self):
        for stage in (1, 2):
            for near in (0, 1):
                for copy in self.copies(stage, near):
                    copy.wait_send()
        self.swap().wait_send()


BIG = 2.0**60


def fold_rows(column):
    row = lax.broadcasted_iota(jnp.int32, (16, 16), 0) & (CAPL - 1)
    col = lax.broadcasted_iota(jnp.int32, (16, 16), 1) & (CAPL - 1)
    same = (row == col).astype(jnp.float32)
    wide = jnp.broadcast_to(column, (16, 128))
    return jnp.dot(
        same, wide, precision=lax.Precision.HIGHEST, preferred_element_type=jnp.float32
    )[:, :1]


def dot(left, right):
    return jnp.dot(left, right, preferred_element_type=jnp.float32)


def split3(value):
    high = value.astype(jnp.bfloat16).astype(jnp.float32)
    rest = value - high
    middle = rest.astype(jnp.bfloat16).astype(jnp.float32)
    return high, middle, rest - middle


def kernel(
    kin, v, wt, q, doc, eid, gain, column, gate_hbm, up_hbm, down_hbm, og_hbm, residual_hbm,
    res_out, routed_out, grads_out, gd_out, ud_out, act_out, dq, dk, dv,
    hbuf, gbuf, kbuf, vbuf, wbbuf, wabuf, gu, down, og, res, perm, perm_t, hx, grads, routed,
    gd, ud, act, pa, pb_, rows, kxe, vxe, qx, gx, ot, top, sb, pb, lb, qs, gs, dqt,
    acc, hid, grd, kx, scat, gain16, column16, pk, pv, ak, ck, bk, ek, av, cv, bv, ev, ah, ch, bh, eh, ai, ci, bi, ei,
    gsend, grecv, glocal, send, recv, tsend, trecv, dsend, drecv, loads, stores,
):
    me = lax.axis_index("ctx")
    tp = lax.axis_index("tp")
    length = q.shape[0]
    heads = q.shape[1] // HD
    scale = HD**-0.5
    factor = scale * LOG2E
    features = down.shape[1]

    fetch_gate = pltpu.make_async_copy(gate_hbm, gu.at[:features], loads.at[0])
    fetch_up = pltpu.make_async_copy(up_hbm, gu.at[features:], loads.at[1])
    fetch_down = pltpu.make_async_copy(down_hbm, down, loads.at[2])
    fetch_og = pltpu.make_async_copy(og_hbm, og, loads.at[3])
    fetch_residual = pltpu.make_async_copy(residual_hbm, res, loads.at[4])
    fetch_residual.start()
    fetch_og.start()
    fetch_gate.start()
    fetch_up.start()
    fetch_down.start()

    y, z, x = place_of()
    signal(at(y, z, 1 - x))
    for d in (1, 3):
        signal(at(y, (z + d) % NZ, x))
        signal(at((y + d) % NY, z, x))
    for d in range(1, TP):
        signal({"tp": (tp + d) % TP})

    quarter = features // 4
    row16 = lax.broadcasted_iota(jnp.int32, (16, length), 0)
    a = lax.broadcasted_iota(jnp.int32, (length, length), 0)
    b = lax.broadcasted_iota(jnp.int32, (length, length), 1)
    before = (a < b).astype(jnp.float32).astype(jnp.bfloat16)

    def in_slot(expert, slot):
        named = jnp.where(eid[...] == expert, 1.0, 0.0)
        rank = dot(named.astype(jnp.bfloat16), before)
        return jnp.where(rank == slot.astype(jnp.float32), named, 0.0)

    mine = in_slot(jnp.broadcast_to(tp, (16, length)), row16 & (CAPL - 1))
    kx[:length, :] = kin[...]
    counts = jnp.sum(jnp.where(doc[...] < row16, 1.0, 0.0), axis=1, keepdims=True)
    kx[length:, :] = jnp.broadcast_to(counts, (16, HD)).astype(jnp.bfloat16)
    fetch_residual.wait()
    fetch_og.wait()
    for src, dst in ((res, hid), (og, grd)):
        picked = jnp.zeros((16, quarter), jnp.float32)
        for i in range(4):
            take = jnp.where((row16 >> 2) == i, mine, 0.0).astype(jnp.bfloat16)
            picked += dot(take, src[:, i * quarter : (i + 1) * quarter])
        dst[...] = picked.astype(jnp.bfloat16)
    pl.semaphore_wait(pltpu.get_barrier_semaphore(), 5 + TP - 1)

    def piece(src, buf, order, i):
        return Gather(src, buf, order, gsend.at[i], grecv.at[i], glocal.at[i])

    moe = [piece(hid, hbuf, 0, 0), piece(grd, gbuf, 1, 1)]
    keys = [piece(kx, kbuf, 0, 2), piece(v, vbuf, 1, 3)]
    weights = [piece(wt.at[:, 384:], wbbuf, 0, 4), piece(wt.at[:, :384], wabuf, 1, 5)]

    def go(parts, step):
        for part in parts:
            if step > 1:
                part.arrive(step - 1)
            if step < 6:
                part.start(step)

    go(moe, 1)
    go(keys, 1)
    go(weights, 1)
    go(moe, 2)
    go(moe, 3)

    def row_of(index):
        token = index & 127
        return (token >> 2) * 16 + (index >> 7) * 4 + (token & 3)

    a = lax.broadcasted_iota(jnp.int32, (512, 512), 0)
    b = lax.broadcasted_iota(jnp.int32, (512, 512), 1)
    perm[...] = (a == row_of(b)).astype(jnp.float32).astype(jnp.bfloat16)
    perm_t[...] = (b == row_of(a)).astype(jnp.float32).astype(jnp.bfloat16)
    row64 = lax.broadcasted_iota(jnp.int32, (64, length), 0)
    placed = in_slot(row64 >> 4, row64 & (CAPL - 1))
    wide16 = lax.broadcasted_iota(jnp.int32, (16, quarter), 0) >> 2
    gain16[...] = jnp.zeros_like(gain16)
    column16[...] = jnp.zeros_like(column16)
    for i in range(4):
        cols = slice(i * quarter, (i + 1) * quarter)
        gain16[...] += jnp.where(wide16 == i, gain[:, cols].astype(jnp.float32), 0.0)
        column16[...] += jnp.where(wide16 == i, column[:, cols].astype(jnp.float32), 0.0)
        scat[i] = jnp.where(((row64 >> 2) & 3) == i, placed, 0.0).T.astype(jnp.bfloat16)
    for h in range(heads):
        cols = slice(h * HD, (h + 1) * HD)
        qs[h * length : (h + 1) * length, :] = q[:, cols]
        qx[h, :HD, :] = q[:, cols].T
        qx[h, HD:, :] = jnp.zeros((HD, length), jnp.bfloat16)
        gx[h, HD:, :] = jnp.zeros((HD, length), jnp.bfloat16)

    go(keys, 2)
    go(moe, 4)
    go(weights, 2)
    go(keys, 3)
    go(moe, 5)
    go(weights, 3)
    go(keys, 4)
    go(weights, 4)
    go(moe, 6)


    def unfold(t, _):
        cols = pl.ds(pl.multiple_of(t * 256, 256), 256)
        block = hbuf[:, :, :, :, cols].reshape(512, 256)
        hx[:, cols] = dot(perm_t[...], block).astype(jnp.bfloat16)
        block = gbuf[:, :, :, :, cols].reshape(512, 256)
        values = dot(perm_t[...], block).astype(jnp.bfloat16)
        for i in range(4):
            grads[:, pl.ds(pl.multiple_of(i * quarter + t * 256, 256), 256)] = values[
                i * 128 : (i + 1) * 128
            ]
        return 0

    lax.fori_loop(0, quarter // 256, unfold, 0)
    total = jnp.zeros((128, 1), jnp.float32)
    for i in range(4):
        x = hx[i * 128 : (i + 1) * 128, :].astype(jnp.float32)
        total += jnp.sum(x * x, axis=1, keepdims=True)
    inverse = lax.rsqrt(total * (1.0 / features) + EPS)
    total = jnp.zeros((128, 1), jnp.float32)
    for i in range(4):
        cols = slice(i * quarter, (i + 1) * quarter)
        x = hx[i * 128 : (i + 1) * 128, :].astype(jnp.float32)
        normed = (x * inverse * gain[:, cols].astype(jnp.float32)).astype(jnp.bfloat16)
        routed[:, cols] = normed
        total += jnp.sum(normed.astype(jnp.float32) * column[:, cols].astype(jnp.float32), axis=1, keepdims=True)
    score = jax.nn.sigmoid(total)
    for i in range(4):
        cols = slice(i * quarter, (i + 1) * quarter)
        routed[:, cols] = (routed[:, cols].astype(jnp.float32) * score).astype(jnp.bfloat16)
    go(keys, 5)
    fetch_gate.wait()
    fetch_up.wait()
    fetch_down.wait()
    gate = dot(routed[...], gu[:features, :])
    upward = dot(routed[...], gu[features:, :])
    active_grad = contract(grads[...], down[...], 1, 1)
    sigma = jax.nn.sigmoid(gate)
    swish = gate * sigma
    act[...] = (swish * upward).astype(jnp.bfloat16)
    gd[...] = (active_grad * upward * sigma * (1.0 + gate * (1.0 - sigma))).astype(jnp.bfloat16)
    ud[...] = (active_grad * swish).astype(jnp.bfloat16)

    def back(t, _):
        first = pl.multiple_of(t * 640, 640)
        values = contract(gd[...], gu[pl.ds(first, 640), :], 1, 1)
        values += contract(ud[...], gu[pl.ds(features + first, 640), :], 1, 1)
        line = pl.multiple_of((t // 2) * 128, 128)
        hx[pl.ds(line, 128), pl.ds(pl.multiple_of((t % 2) * 640, 640), 640)] = values.astype(
            jnp.bfloat16
        )
        return 0

    lax.fori_loop(0, 8, back, 0)

    def fold(t, _):
        cols = pl.ds(pl.multiple_of(t * 128, 128), 128)
        block = dot(perm[...], hx[:, cols]).astype(jnp.bfloat16)
        pa[:, :, :, :, cols] = block.reshape(NY, NZ, NX, 16, 128)
        cols = pl.ds(pl.multiple_of(quarter // 2 + t * 128, 128), 128)
        block = dot(perm[...], hx[:, cols]).astype(jnp.bfloat16)
        cols = pl.ds(pl.multiple_of(t * 128, 128), 128)
        pb_[:, :, :, :, cols] = block.reshape(NY, NZ, NX, 16, 128)
        return 0

    lax.fori_loop(0, quarter // 256, fold, 0)
    expert_sums = [
        Scatter(pa, ah, ch, bh, eh, 0, send.at[0], recv.at[0]),
        Scatter(pb_, ai, ci, bi, ei, 1, send.at[1], recv.at[1]),
    ]
    for part_ in expert_sums:
        part_.far(1)
    saves = [
        pltpu.make_async_copy(src, dst, stores.at[i])
        for i, (src, dst) in enumerate(
            [(routed, routed_out), (grads, grads_out), (gd, gd_out), (ud, ud_out), (act, act_out)]
        )
    ]
    for save in saves:
        save.start()
    for part_ in expert_sums:
        part_.near(1)
    go(keys, 6)

    counts = jnp.sum(kbuf[:, :, :, length:, :].astype(jnp.float32), axis=(0, 1, 2))[:8]
    a = lax.broadcasted_iota(jnp.int32, (8, HD), 0)
    b = lax.broadcasted_iota(jnp.int32, (8, HD), 1)
    starts = jnp.sum(jnp.where(a == b, counts, 0.0), axis=0, keepdims=True)
    ends = jnp.sum(jnp.where(a == b + 1, counts, 0.0), axis=0, keepdims=True)
    lane = lax.broadcasted_iota(jnp.int32, (1, HD), 1)
    ends = jnp.where(lane == 7, float(CTX * length), ends)
    token = lax.broadcasted_iota(jnp.int32, (length, HD), 0).astype(jnp.float32)
    ones_at = (lane >= 8) & (lane < 11)
    ones_row = jnp.where(ones_at, 1.0, 0.0)
    ones_block = jnp.broadcast_to(ones_row, (length, HD)).astype(jnp.bfloat16)

    def extend(j, _):
        y, z, x = j // (NZ * NX), (j // NX) % NZ, j % NX
        lines = pl.ds(pl.multiple_of(j * length, length), length)
        first = (j * length).astype(jnp.float32)
        inside = (token >= starts - first) & (token < ends - first)
        kxe[lines, :HD] = kbuf[y, z, x, :length, :]
        kxe[lines, HD:] = jnp.where(inside, -BIG, ones_row).astype(jnp.bfloat16)
        vxe[lines, :HD] = vbuf[y, z, x]
        vxe[lines, HD:] = ones_block
        return 0

    lax.fori_loop(0, me + 1, extend, 0)
    other = jnp.where((row16 < 8) & (row16 != doc[...]), 1.0, 0.0)
    for h in range(heads):
        qx[h, HD : HD + 16, :] = other.astype(jnp.bfloat16)
    key_id = lax.broadcasted_iota(jnp.int32, (length, length), 0)
    query_id = lax.broadcasted_iota(jnp.int32, (length, length), 1)
    ones16 = jnp.ones((16, length), jnp.bfloat16)

    def forward(j, diagonal):
        lines = pl.ds(pl.multiple_of(j * length, length), length)
        key = kxe[lines, :]
        value_t = jnp.concatenate([vxe[lines, :HD].T, ones16], axis=0)
        tops, shrinks = [], []
        for h in range(heads):
            logits = dot(key, qx[h])
            if diagonal:
                logits = jnp.where(key_id <= query_id, logits, -BIG)
            sb[:, h * length : (h + 1) * length] = logits
            new = jnp.max(logits, axis=0, keepdims=True)
            if not diagonal:
                old = top[h]
                new = jnp.maximum(old, new)
                shrinks.append(jnp.exp2((old - new) * factor))
            top[h] = new
            tops.append(new * factor)
        for h in range(heads):
            cols = slice(h * length, (h + 1) * length)
            pb[:, cols] = jnp.exp2(sb[:, cols] * factor - tops[h]).astype(jnp.bfloat16)
        for h in range(heads):
            more = dot(value_t, pb[:, h * length : (h + 1) * length])
            ot[h] = more if diagonal else ot[h] * shrinks[h] + more

    def forward_step(i, _):
        forward(me - i, False)
        return 0

    def forward_part(k):
        lax.fori_loop(1 + me * k // 5, 1 + me * (k + 1) // 5, forward_step, 0)

    forward(me, True)
    forward_part(0)
    for part_ in expert_sums:
        part_.own(1)
        part_.far(2)
    forward_part(1)
    for part_ in expert_sums:
        part_.near(2)
    go(weights, 5)
    forward_part(2)
    for part_ in expert_sums:
        part_.own(2)
        part_.last()
    forward_part(3)

    routed_grad = jnp.concatenate([part_.total() for part_ in expert_sums], axis=1)
    hidden = hid[...].astype(jnp.float32)
    inverse = lax.rsqrt(
        fold_rows(jnp.sum(hidden * hidden, axis=1, keepdims=True)) * (1.0 / features) + EPS
    )
    normed = (hidden * inverse * gain16[...]).astype(jnp.bfloat16).astype(jnp.float32)
    score = jax.nn.sigmoid(fold_rows(jnp.sum(normed * column16[...], axis=1, keepdims=True)))
    dots = fold_rows(jnp.sum(routed_grad * normed, axis=1, keepdims=True))
    score_grad = dots * score * (1.0 - score)
    scaled = gain16[...] * (routed_grad * score + score_grad * column16[...])
    mean = fold_rows(jnp.sum(scaled * hidden, axis=1, keepdims=True)) * (1.0 / features)
    own_rows = inverse * scaled - hidden * (inverse * inverse * inverse) * mean
    rows[tp] = own_rows.astype(jnp.bfloat16)

    def swap(d, source):
        return remote(
            rows.at[source], rows.at[source], tsend.at[d], trecv.at[d], {"tp": (tp + d) % TP}
        )

    for d in range(1, TP):
        swap(d, tp).start()
    forward_part(4)

    for d in range(1, TP):
        swap(d, (tp + TP - d) % TP).wait_recv()

    for i in range(4):

        def add(t, _, i=i):
            cols = pl.ds(pl.multiple_of(t * 256, 256), 256)
            wide = pl.ds(pl.multiple_of(i * quarter + t * 256, 256), 256)
            more = dot(scat[i], rows[:, :, cols].reshape(TP * 16, 256))
            res[:, wide] = (og[:, wide].astype(jnp.float32) + more).astype(jnp.bfloat16)
            return 0

        lax.fori_loop(0, quarter // 256, add, 0)
    save_res = pltpu.make_async_copy(res, res_out, stores.at[5])
    save_res.start()

    go(weights, 6)
    acc[...] = jnp.zeros_like(acc)

    def project(i, _):
        y, z = i // 2, (i % 2) * 2
        left = res[:, pl.ds(pl.multiple_of(i * 640, 640), 640)]
        acc[:, :384] += dot(left, wabuf[y, pl.ds(z, 2)].reshape(640, 384))
        acc[:, 384:] += dot(left, wbbuf[y, pl.ds(z, 2)].reshape(640, 256))
        return 0

    lax.fori_loop(0, 8, project, 0)
    for h in range(heads):
        grad = acc[:, h * HD : (h + 1) * HD].astype(jnp.bfloat16)
        gs[h * length : (h + 1) * length, :] = grad
        grad_t = grad.T
        gx[h, :HD, :] = grad_t
        total = ot[h, HD : HD + 1, :]
        delta = jnp.sum(ot[h, :HD, :] * grad_t.astype(jnp.float32), axis=0, keepdims=True) / total
        high, middle, rest = split3(-delta)
        extra = jnp.where(row16 == 8, high, 0.0)
        extra = jnp.where(row16 == 9, middle, extra)
        extra = jnp.where(row16 == 10, rest, extra)
        gx[h, HD : HD + 16, :] = extra.astype(jnp.bfloat16)
        high, middle, rest = split3(-(top[h] + jnp.log2(total) * (1.0 / factor)))
        extra = jnp.where(row16 == 8, high, other)
        extra = jnp.where(row16 == 9, middle, extra)
        extra = jnp.where(row16 == 10, rest, extra)
        qx[h, HD : HD + 16, :] = extra.astype(jnp.bfloat16)

    def backward(j, diagonal):
        lines = pl.ds(pl.multiple_of(j * length, length), length)
        key = kxe[lines, :]
        key_t = kxe[lines, :HD].T
        value = vxe[lines, :]
        for h in range(heads):
            cols = slice(h * length, (h + 1) * length)
            logits = dot(key, qx[h])
            if diagonal:
                logits = jnp.where(key_id <= query_id, logits, -BIG)
            prob = jnp.exp2(logits * factor)
            lb[:, cols] = (prob * dot(value, gx[h])).astype(jnp.bfloat16)
            pb[:, cols] = prob.astype(jnp.bfloat16)
        value_sum = dot(pb[...], gs[...])
        key_sum = dot(lb[...], qs[...]) * scale
        for h in range(heads):
            more = dot(key_t, lb[:, h * length : (h + 1) * length])
            dqt[h] = dqt[h] + more
        y, z, x = j // (NZ * NX), (j // NX) % NZ, j % NX
        pk[y, z, x] = key_sum.astype(jnp.bfloat16)
        pv[y, z, x] = value_sum.astype(jnp.bfloat16)

    sums = [
        Scatter(pk, ak, ck, bk, ek, 0, dsend.at[0], drecv.at[0]),
        Scatter(pv, av, cv, bv, ev, 1, dsend.at[1], drecv.at[1]),
    ]
    y, z, x = place_of()
    for h in range(heads):
        dqt[h] = jnp.zeros((HD, length), jnp.float32)

    def backward_step(i, _):
        r = jnp.where(i < 14, i - 8, i - 14)
        turn = jnp.where(i < 14, r // 2, r // 6)
        to_y = (y + 3 - 2 * turn + turn // 2) % NY
        turn = (r % 6) // 2
        to_z = (z + 3 - 2 * turn + turn // 2) % NZ
        to_y = jnp.where(i < 8, (y + 2) % NY, to_y)
        to_z = jnp.where(i < 8, i // 2, jnp.where(i < 14, (z + 2) % NZ, to_z))
        j = to_y * (NZ * NX) + to_z * NX + i % 2

        @pl.when(j < me)
        def _():
            backward(j, False)

        @pl.when(j == me)
        def _():
            backward(j, True)

        @pl.when(j > me)
        def _():
            pk[to_y, to_z, i % 2] = jnp.zeros((length, HD), jnp.bfloat16)
            pv[to_y, to_z, i % 2] = jnp.zeros((length, HD), jnp.bfloat16)

        @pl.when(i == 7)
        def _():
            sums[0].far(1)

        @pl.when(i == 13)
        def _():
            sums[1].far(1)

        @pl.when(i == 25)
        def _():
            sums[0].near(1)

        @pl.when(i == 29)
        def _():
            sums[1].near(1)

        return 0

    lax.fori_loop(0, CTX, backward_step, 0)
    for part_ in sums:
        part_.own(1)
        part_.far(2)
    for h in range(heads):
        dq[:, h * HD : (h + 1) * HD] = (dqt[h].T * scale).astype(jnp.bfloat16)
    for part_ in sums:
        part_.near(2)
    for part_ in sums:
        part_.own(2)
        part_.last()
    dk[...] = sums[0].total().astype(jnp.bfloat16)
    dv[...] = sums[1].total().astype(jnp.bfloat16)
    for part_ in sums:
        part_.finish()

    for part_ in expert_sums:
        part_.finish()
    for d in range(1, TP):
        swap(d, tp).wait_send()
    for piece_ in moe + keys + weights:
        piece_.finish()
    for save in saves:
        save.wait()
    save_res.wait()


def fused(kin, v, wt, q, doc, eid, gain, column, gate, up, down, og, residual):
    length, width = q.shape
    heads = width // HD
    features = down.shape[1]
    rows = CTX * CAPL
    hidden = gate.shape[1]
    bf16, f32 = jnp.bfloat16, jnp.float32

    def shape(*dims):
        return jax.ShapeDtypeStruct(dims, bf16)

    vmem = pl.BlockSpec(memory_space=pltpu.VMEM)
    hbm = pl.BlockSpec(memory_space=pl.ANY)
    return pl.pallas_call(
        kernel,
        out_shape=[
            shape(length, features),
            shape(rows, features),
            shape(rows, features),
            shape(rows, hidden),
            shape(rows, hidden),
            shape(rows, hidden),
            shape(length, width),
            shape(length, HD),
            shape(length, HD),
        ],
        in_specs=[vmem] * 8 + [hbm] * 5,
        out_specs=[hbm] * 6 + [vmem] * 3,
        scratch_shapes=[
            pltpu.VMEM((NY, NZ, NX) + (16, features // 4), bf16),
            pltpu.VMEM((NY, NZ, NX) + (16, features // 4), bf16),
            pltpu.VMEM((NY, NZ, NX) + (length + 16, HD), bf16),
            pltpu.VMEM((NY, NZ, NX) + v.shape, bf16),
            pltpu.VMEM((NY, NZ, NX) + (wt.shape[0], 256), bf16),
            pltpu.VMEM((NY, NZ, NX) + (wt.shape[0], 384), bf16),
            pltpu.VMEM((2 * features, hidden), bf16),
            pltpu.VMEM((hidden, features), bf16),
            pltpu.VMEM((length, features), bf16),
            pltpu.VMEM((length, features), bf16),
            pltpu.VMEM((512, 512), bf16),
            pltpu.VMEM((512, 512), bf16),
            pltpu.VMEM((512, features // 4), bf16),
            pltpu.VMEM((rows, features), bf16),
            pltpu.VMEM((rows, features), bf16),
            pltpu.VMEM((rows, hidden), bf16),
            pltpu.VMEM((rows, hidden), bf16),
            pltpu.VMEM((rows, hidden), bf16),
            pltpu.VMEM((NY, NZ, NX, 16, features // 8), bf16),
            pltpu.VMEM((NY, NZ, NX, 16, features // 8), bf16),
            pltpu.VMEM((TP, 16, features // 4), bf16),
            pltpu.VMEM((CTX * length, 2 * HD), bf16),
            pltpu.VMEM((CTX * length, 2 * HD), bf16),
            pltpu.VMEM((heads, 2 * HD, length), bf16),
            pltpu.VMEM((heads, 2 * HD, length), bf16),
            pltpu.VMEM((heads, HD + 16, length), f32),
            pltpu.VMEM((heads, 1, length), f32),
            pltpu.VMEM((length, heads * length), f32),
            pltpu.VMEM((length, heads * length), bf16),
            pltpu.VMEM((length, heads * length), bf16),
            pltpu.VMEM((heads * length, HD), bf16),
            pltpu.VMEM((heads * length, HD), bf16),
            pltpu.VMEM((heads, HD, length), f32),
            pltpu.VMEM((length, width), f32),
            pltpu.VMEM((16, features // 4), bf16),
            pltpu.VMEM((16, features // 4), bf16),
            pltpu.VMEM((length + 16, HD), bf16),
            pltpu.VMEM((4, length, 64), bf16),
            pltpu.VMEM((16, features // 4), f32),
            pltpu.VMEM((16, features // 4), f32),
            pltpu.VMEM((NY, NZ, NX, length, HD), bf16),
            pltpu.VMEM((NY, NZ, NX, length, HD), bf16),
            pltpu.VMEM((2, 2, 2, length, HD), bf16),
            pltpu.VMEM((2, 4, 2, length, HD), bf16),
            pltpu.VMEM((3, 1, length, HD), bf16),
            pltpu.VMEM((2, 2, length, HD), bf16),
            pltpu.VMEM((2, 2, 2, length, HD), bf16),
            pltpu.VMEM((2, 4, 2, length, HD), bf16),
            pltpu.VMEM((3, 1, length, HD), bf16),
            pltpu.VMEM((2, 2, length, HD), bf16),
            pltpu.VMEM((2, 2, 2, 16, features // 8), bf16),
            pltpu.VMEM((2, 4, 2, 16, features // 8), bf16),
            pltpu.VMEM((3, 1, 16, features // 8), bf16),
            pltpu.VMEM((2, 2, 16, features // 8), bf16),
            pltpu.VMEM((2, 2, 2, 16, features // 8), bf16),
            pltpu.VMEM((2, 4, 2, 16, features // 8), bf16),
            pltpu.VMEM((3, 1, 16, features // 8), bf16),
            pltpu.VMEM((2, 2, 16, features // 8), bf16),
            pltpu.SemaphoreType.DMA((6, 9)),
            pltpu.SemaphoreType.DMA((6, 9)),
            pltpu.SemaphoreType.DMA((6,)),
            pltpu.SemaphoreType.DMA((2, 9)),
            pltpu.SemaphoreType.DMA((2, 9)),
            pltpu.SemaphoreType.DMA((TP,)),
            pltpu.SemaphoreType.DMA((TP,)),
            pltpu.SemaphoreType.DMA((2, 9)),
            pltpu.SemaphoreType.DMA((2, 9)),
            pltpu.SemaphoreType.DMA((5,)),
            pltpu.SemaphoreType.DMA((6,)),
        ],
        compiler_params=pltpu.CompilerParams(
            collective_id=1, has_side_effects=True, vmem_limit_bytes=60 << 20
        ),
    )(kin, v, wt, q, doc, eid, gain, column, gate, up, down, og, residual)


def local(
    residual,
    out_grad,
    queries,
    key_rows,
    value_rows,
    doc_ids,
    expert_ids,
    norm_gain,
    router_columns,
    gate_weight,
    up_weight,
    down_weight,
    out_weight,
):
    residual_grad, routed, grads, gate_delta, up_delta, active, query_grad, key_grad, value_grad = fused(
        key_rows,
        value_rows,
        out_weight.T,
        queries,
        doc_ids[None, :],
        expert_ids[None, :],
        norm_gain[None, :],
        router_columns.reshape(1, -1),
        gate_weight[0],
        up_weight[0],
        down_weight[0],
        out_grad,
        residual,
    )
    grad_gate = contract(routed, gate_delta, 0, 0).astype(jnp.bfloat16)
    grad_up = contract(routed, up_delta, 0, 0).astype(jnp.bfloat16)
    grad_down = contract(active, grads, 0, 0).astype(jnp.bfloat16)
    return (
        residual_grad, query_grad, key_grad, value_grad, grad_gate[None], grad_up[None], grad_down[None]
    )


def solution(mesh):
    in_specs = (
        P("ctx", None),
        P("ctx", None),
        P("ctx", "tp"),
        P("ctx", "tp"),
        P("ctx", "tp"),
        P("ctx"),
        P("ctx"),
        P(),
        P(None, "tp"),
        P("tp", None, "ctx"),
        P("tp", None, "ctx"),
        P("tp", "ctx", None),
        P("tp", "ctx"),
    )
    out_specs = (
        P("ctx", None),
        P("ctx", "tp"),
        P("ctx", "tp"),
        P("ctx", "tp"),
        P("tp", None, "ctx"),
        P("tp", None, "ctx"),
        P("tp", "ctx", None),
    )
    return jax.shard_map(local, mesh=mesh, in_specs=in_specs, out_specs=out_specs, check_vma=False)
```

```python
import jax
import jax.numpy as jnp
from jax import lax
from jax.experimental import pallas as pl
from jax.experimental.pallas import tpu as pltpu
from jax.sharding import PartitionSpec as P

HD = 128
CAPL = 4
EPS = 1e-05
NEG = -1e30
LOG2E = 1.4426950408889634
MESH = pl.DeviceIdType.MESH
NY, NZ, NX = 4, 4, 2
CTX = NY * NZ * NX
TP = 4


def contract(left, right, left_dim, right_dim):
    return lax.dot_general(
        left, right, (((left_dim,), (right_dim,)), ((), ())), preferred_element_type=jnp.float32
    )


def place_of():
    me = lax.axis_index("ctx")
    return me // (NZ * NX), (me // NX) % NZ, me % NX


def at(y, z, x):
    return {"ctx": y * (NZ * NX) + z * NX + x}


def signal(device):
    pl.semaphore_signal(
        pltpu.get_barrier_semaphore(), inc=1, device_id=device, device_id_type=MESH
    )


def remote(src, dst, send, recv, device):
    return pltpu.make_async_remote_copy(
        src_ref=src, dst_ref=dst, send_sem=send, recv_sem=recv, device_id=device, device_id_type=MESH
    )


class Gather:
    def __init__(self, src, buf, order, send, recv, local):
        self.src, self.buf, self.order = src, buf, order
        self.send, self.recv, self.local = send, recv, local

    def copy(self, src, dst, k, device):
        return remote(src, dst, self.send.at[k], self.recv.at[k], device)

    def along_z(self, step):
        return (self.order == 0) == (step in (2, 3))

    def slab(self, step, offset, half):
        y, z, x = place_of()
        buf = self.buf
        if self.along_z(step):
            z = (z + offset) % NZ
        else:
            y = (y + offset) % NY
        if step in (2, 3):
            return buf.at[y, z] if half is None else buf.at[y, z, half]
        if self.along_z(step):
            return buf.at[:, z] if half is None else buf.at[2 * half : 2 * half + 2, z]
        return buf.at[y] if half is None else buf.at[y, 2 * half : 2 * half + 2]

    def device(self, step, offset):
        y, z, x = place_of()
        if self.along_z(step):
            return at(y, (z + offset) % NZ, x)
        return at((y + offset) % NY, z, x)

    def sends(self, step):
        y, z, x = place_of()
        if step == 1:
            return [self.copy(self.src, self.buf.at[y, z, x], 0, at(y, z, 1 - x))]
        copies = []
        for i, d in enumerate((1, 3)):
            k = 1 + 2 * (step - 2) + i
            part = self.slab(step, 0, None) if step in (2, 4) else self.slab(step, 4 - d, i)
            copies.append(self.copy(part, part, k, self.device(step, d)))
        return copies

    def receives(self, step):
        y, z, x = place_of()
        if step == 1:
            part = self.buf.at[y, z, 1 - x]
            return [self.copy(part, part, 0, at(y, z, 1 - x))]
        copies = []
        for i, d in enumerate((1, 3)):
            k = 1 + 2 * (step - 2) + i
            part = self.slab(step, 4 - d, None) if step in (2, 4) else self.slab(step, 2, i)
            copies.append(self.copy(part, part, k, self.device(step, d)))
        return copies

    def own(self):
        y, z, x = place_of()
        return pltpu.make_async_copy(self.src, self.buf.at[y, z, x], self.local)

    def start(self, step):
        if step == 1:
            self.own().start()
        for copy in self.sends(step):
            copy.start()

    def arrive(self, step):
        if step == 1:
            self.own().wait()
        for copy in self.receives(step):
            copy.wait_recv()

    def finish(self):
        for step in range(1, 6):
            for copy in self.sends(step):
                copy.wait_send()


class Scatter:
    def __init__(self, p, a1, c1, a2, c2, order, send, recv):
        self.p, self.order, self.send, self.recv = p, order, send, recv
        self.far_in, self.near_in = (a1, a2), (c1, c2)

    def along_z(self, stage):
        return (self.order == 0) == (stage == 2)

    def slab(self, stage, offset, half):
        y, z, x = place_of()
        p = self.p
        if self.along_z(stage):
            z = (z + offset) % NZ
        else:
            y = (y + offset) % NY
        if stage == 2:
            return p.at[y, z] if half is None else p.at[y, z, half : half + 1]
        if self.along_z(stage):
            return p.at[:, z] if half is None else p.at[2 * half : 2 * half + 2, z]
        return p.at[y] if half is None else p.at[y, 2 * half : 2 * half + 2]

    def device(self, stage, offset):
        y, z, x = place_of()
        if self.along_z(stage):
            return at(y, (z + offset) % NZ, x)
        return at((y + offset) % NY, z, x)

    def copies(self, stage, near):
        result = []
        for i, d in enumerate((1, 3)):
            k = 4 * (stage - 1) + 2 * near + i
            if near:
                src, dst = self.slab(stage, d, None), self.near_in[stage - 1].at[i]
            else:
                src, dst = self.slab(stage, 2, i), self.far_in[stage - 1].at[i]
            result.append(remote(src, dst, self.send.at[k], self.recv.at[k], self.device(stage, d)))
        return result

    def far(self, stage):
        for copy in self.copies(stage, 0):
            copy.start()

    def near(self, stage):
        for i, (d, copy) in enumerate(zip((1, 3), self.copies(stage, 0))):
            copy.wait_recv()
            half = self.slab(stage, d, i)
            more = self.far_in[stage - 1][i].astype(jnp.float32)
            half[...] = (half[...].astype(jnp.float32) + more).astype(jnp.bfloat16)
        for copy in self.copies(stage, 1):
            copy.start()

    def own(self, stage):
        for copy in self.copies(stage, 1):
            copy.wait_recv()
        slab = self.slab(stage, 0, None)
        arrived = self.near_in[stage - 1]
        more = arrived[0].astype(jnp.float32) + arrived[1].astype(jnp.float32)
        slab[...] = (slab[...].astype(jnp.float32) + more).astype(jnp.bfloat16)

    def swap(self):
        y, z, x = place_of()
        there = self.far_in[1].at[2]
        return remote(
            self.p.at[y, z, 1 - x], there.at[0], self.send.at[8], self.recv.at[8], at(y, z, 1 - x)
        )

    def last(self):
        self.swap().start()

    def total(self):
        y, z, x = place_of()
        self.swap().wait_recv()
        return self.p[y, z, x].astype(jnp.float32) + self.far_in[1][2, 0].astype(jnp.float32)

    def finish(self):
        for stage in (1, 2):
            for near in (0, 1):
                for copy in self.copies(stage, near):
                    copy.wait_send()
        self.swap().wait_send()


class Share(Scatter):
    def pair(self, d):
        y, z, x = place_of()
        inner = (z if self.order == 0 else y) * 2 + x
        to, source = (inner + d) % 8, (inner + 8 - d) % 8
        if self.order == 0:
            src, there = self.p.at[y, to // 2, to % 2], at(y, to // 2, to % 2)
        else:
            src, there = self.p.at[to // 2, z, to % 2], at(to // 2, z, to % 2)
        return remote(
            src, self.far_in[1].at[d], self.send.at[4 + d], self.recv.at[4 + d], there
        )

    def spread(self):
        for d in range(1, 8):
            self.pair(d).start()

    def total(self):
        y, z, x = place_of()
        total = self.p[y, z, x].astype(jnp.float32)
        for d in range(1, 8):
            self.pair(d).wait_recv()
            total += self.far_in[1][d].astype(jnp.float32)
        return total

    def finish(self):
        for near in (0, 1):
            for copy in self.copies(1, near):
                copy.wait_send()
        for d in range(1, 8):
            self.pair(d).wait_send()


BIG = 2.0**60


def fold_rows(column):
    row = lax.broadcasted_iota(jnp.int32, (16, 16), 0) & (CAPL - 1)
    col = lax.broadcasted_iota(jnp.int32, (16, 16), 1) & (CAPL - 1)
    same = (row == col).astype(jnp.float32)
    wide = jnp.broadcast_to(column, (16, 128))
    return jnp.dot(
        same, wide, precision=lax.Precision.HIGHEST, preferred_element_type=jnp.float32
    )[:, :1]


def dot(left, right):
    return jnp.dot(left, right, preferred_element_type=jnp.float32)


def split3(value):
    high = value.astype(jnp.bfloat16).astype(jnp.float32)
    rest = value - high
    middle = rest.astype(jnp.bfloat16).astype(jnp.float32)
    return high, middle, rest - middle


def kernel(
    kin, v, wt, q, doc, eid, gain, column, gate_hbm, up_hbm, down_hbm, og_hbm, residual_hbm,
    res_out, routed_out, grads_out, gd_out, ud_out, act_out, dq, dk, dv,
    hbuf, gbuf, kbuf, vbuf, wbbuf, wabuf, gu, down, og, res, perm, perm_t, hx, grads, routed,
    gd, ud, act, pa, pb_, rows, kxe, vxe, qx, gx, ot, top, sb, pb, lb, qs, gs, dqt,
    acc, hid, grd, kx, scat, gain16, column16, pk, pv, ak, ck, bk, av, cv, bv, ah, ch, bh, eh, ai, ci, bi, ei,
    gsend, grecv, glocal, send, recv, tsend, trecv, dsend, drecv, loads, stores,
):
    me = lax.axis_index("ctx")
    tp = lax.axis_index("tp")
    length = q.shape[0]
    heads = q.shape[1] // HD
    scale = HD**-0.5
    factor = scale * LOG2E
    features = down.shape[1]

    fetch_gate = pltpu.make_async_copy(gate_hbm, gu.at[:features], loads.at[0])
    fetch_up = pltpu.make_async_copy(up_hbm, gu.at[features:], loads.at[1])
    fetch_down = pltpu.make_async_copy(down_hbm, down, loads.at[2])
    fetch_og = pltpu.make_async_copy(og_hbm, og, loads.at[3])
    fetch_residual = pltpu.make_async_copy(residual_hbm, res, loads.at[4])
    fetch_residual.start()
    fetch_og.start()
    fetch_gate.start()
    fetch_up.start()
    fetch_down.start()

    y, z, x = place_of()
    for d in range(1, 8):
        to = (z * 2 + x + d) % 8
        signal(at(y, to // 2, to % 2))
    for d in range(1, 4):
        for e in (0, 1):
            signal(at((y + d) % NY, z, (x + e) % 2))
    for d in range(1, TP):
        signal({"tp": (tp + d) % TP})

    quarter = features // 4
    row16 = lax.broadcasted_iota(jnp.int32, (16, length), 0)
    a = lax.broadcasted_iota(jnp.int32, (length, length), 0)
    b = lax.broadcasted_iota(jnp.int32, (length, length), 1)
    before = (a < b).astype(jnp.float32).astype(jnp.bfloat16)

    def in_slot(expert, slot):
        named = jnp.where(eid[...] == expert, 1.0, 0.0)
        rank = dot(named.astype(jnp.bfloat16), before)
        return jnp.where(rank == slot.astype(jnp.float32), named, 0.0)

    mine = in_slot(jnp.broadcast_to(tp, (16, length)), row16 & (CAPL - 1))
    kx[:length, :] = kin[...]
    counts = jnp.sum(jnp.where(doc[...] < row16, 1.0, 0.0), axis=1, keepdims=True)
    kx[length:, :] = jnp.broadcast_to(counts, (16, HD)).astype(jnp.bfloat16)
    fetch_residual.wait()
    fetch_og.wait()
    for src, dst in ((res, hid), (og, grd)):
        picked = jnp.zeros((16, quarter), jnp.float32)
        for i in range(4):
            take = jnp.where((row16 >> 2) == i, mine, 0.0).astype(jnp.bfloat16)
            picked += dot(take, src[:, i * quarter : (i + 1) * quarter])
        dst[...] = picked.astype(jnp.bfloat16)
    pl.semaphore_wait(pltpu.get_barrier_semaphore(), 13 + TP - 1)

    def piece(src, buf, order, i):
        return Gather(src, buf, order, gsend.at[i], grecv.at[i], glocal.at[i])

    moe = [piece(hid, hbuf, 0, 0), piece(grd, gbuf, 1, 1)]
    keys = [piece(kx, kbuf, 0, 2), piece(v, vbuf, 1, 3)]
    weights = [piece(wt.at[:, 384:], wbbuf, 0, 4), piece(wt.at[:, :384], wabuf, 1, 5)]

    def go(parts, step):
        for part in parts:
            if step > 1:
                part.arrive(step - 1)
            if step < 6:
                part.start(step)

    go(moe, 1)
    go(keys, 1)
    go(weights, 1)
    go(moe, 2)
    go(moe, 3)

    def row_of(index):
        token = index & 127
        return (token >> 2) * 16 + (index >> 7) * 4 + (token & 3)

    a = lax.broadcasted_iota(jnp.int32, (512, 512), 0)
    b = lax.broadcasted_iota(jnp.int32, (512, 512), 1)
    perm[...] = (a == row_of(b)).astype(jnp.float32).astype(jnp.bfloat16)
    perm_t[...] = (b == row_of(a)).astype(jnp.float32).astype(jnp.bfloat16)
    row64 = lax.broadcasted_iota(jnp.int32, (64, length), 0)
    placed = in_slot(row64 >> 4, row64 & (CAPL - 1))
    wide16 = lax.broadcasted_iota(jnp.int32, (16, quarter), 0) >> 2
    gain16[...] = jnp.zeros_like(gain16)
    column16[...] = jnp.zeros_like(column16)
    for i in range(4):
        cols = slice(i * quarter, (i + 1) * quarter)
        gain16[...] += jnp.where(wide16 == i, gain[:, cols].astype(jnp.float32), 0.0)
        column16[...] += jnp.where(wide16 == i, column[:, cols].astype(jnp.float32), 0.0)
        scat[i] = jnp.where(((row64 >> 2) & 3) == i, placed, 0.0).T.astype(jnp.bfloat16)
    for h in range(heads):
        cols = slice(h * HD, (h + 1) * HD)
        qs[h * length : (h + 1) * length, :] = q[:, cols]
        qx[h, :HD, :] = q[:, cols].T
        qx[h, HD:, :] = jnp.zeros((HD, length), jnp.bfloat16)
        gx[h, HD:, :] = jnp.zeros((HD, length), jnp.bfloat16)

    go(keys, 2)
    go(moe, 4)
    go(weights, 2)
    go(keys, 3)
    go(moe, 5)
    go(weights, 3)
    go(keys, 4)
    go(weights, 4)
    go(moe, 6)


    def unfold(t, _):
        cols = pl.ds(pl.multiple_of(t * 256, 256), 256)
        block = hbuf[:, :, :, :, cols].reshape(512, 256)
        hx[:, cols] = dot(perm_t[...], block).astype(jnp.bfloat16)
        block = gbuf[:, :, :, :, cols].reshape(512, 256)
        values = dot(perm_t[...], block).astype(jnp.bfloat16)
        for i in range(4):
            grads[:, pl.ds(pl.multiple_of(i * quarter + t * 256, 256), 256)] = values[
                i * 128 : (i + 1) * 128
            ]
        return 0

    lax.fori_loop(0, quarter // 256, unfold, 0)
    total = jnp.zeros((128, 1), jnp.float32)
    for i in range(4):
        x = hx[i * 128 : (i + 1) * 128, :].astype(jnp.float32)
        total += jnp.sum(x * x, axis=1, keepdims=True)
    inverse = lax.rsqrt(total * (1.0 / features) + EPS)
    total = jnp.zeros((128, 1), jnp.float32)
    for i in range(4):
        cols = slice(i * quarter, (i + 1) * quarter)
        x = hx[i * 128 : (i + 1) * 128, :].astype(jnp.float32)
        normed = (x * inverse * gain[:, cols].astype(jnp.float32)).astype(jnp.bfloat16)
        routed[:, cols] = normed
        total += jnp.sum(normed.astype(jnp.float32) * column[:, cols].astype(jnp.float32), axis=1, keepdims=True)
    score = jax.nn.sigmoid(total)
    for i in range(4):
        cols = slice(i * quarter, (i + 1) * quarter)
        routed[:, cols] = (routed[:, cols].astype(jnp.float32) * score).astype(jnp.bfloat16)
    go(keys, 5)
    fetch_gate.wait()
    fetch_up.wait()
    fetch_down.wait()
    gate = dot(routed[...], gu[:features, :])
    upward = dot(routed[...], gu[features:, :])
    active_grad = contract(grads[...], down[...], 1, 1)
    sigma = jax.nn.sigmoid(gate)
    swish = gate * sigma
    act[...] = (swish * upward).astype(jnp.bfloat16)
    gd[...] = (active_grad * upward * sigma * (1.0 + gate * (1.0 - sigma))).astype(jnp.bfloat16)
    ud[...] = (active_grad * swish).astype(jnp.bfloat16)

    def back(t, _):
        first = pl.multiple_of(t * 640, 640)
        values = contract(gd[...], gu[pl.ds(first, 640), :], 1, 1)
        values += contract(ud[...], gu[pl.ds(features + first, 640), :], 1, 1)
        line = pl.multiple_of((t // 2) * 128, 128)
        hx[pl.ds(line, 128), pl.ds(pl.multiple_of((t % 2) * 640, 640), 640)] = values.astype(
            jnp.bfloat16
        )
        return 0

    lax.fori_loop(0, 8, back, 0)

    def fold(t, _):
        cols = pl.ds(pl.multiple_of(t * 128, 128), 128)
        block = dot(perm[...], hx[:, cols]).astype(jnp.bfloat16)
        pa[:, :, :, :, cols] = block.reshape(NY, NZ, NX, 16, 128)
        cols = pl.ds(pl.multiple_of(quarter // 2 + t * 128, 128), 128)
        block = dot(perm[...], hx[:, cols]).astype(jnp.bfloat16)
        cols = pl.ds(pl.multiple_of(t * 128, 128), 128)
        pb_[:, :, :, :, cols] = block.reshape(NY, NZ, NX, 16, 128)
        return 0

    lax.fori_loop(0, quarter // 256, fold, 0)
    expert_sums = [
        Scatter(pa, ah, ch, bh, eh, 0, send.at[0], recv.at[0]),
        Scatter(pb_, ai, ci, bi, ei, 1, send.at[1], recv.at[1]),
    ]
    for part_ in expert_sums:
        part_.far(1)
    saves = [
        pltpu.make_async_copy(src, dst, stores.at[i])
        for i, (src, dst) in enumerate(
            [(routed, routed_out), (grads, grads_out), (gd, gd_out), (ud, ud_out), (act, act_out)]
        )
    ]
    for save in saves:
        save.start()
    for part_ in expert_sums:
        part_.near(1)
    go(keys, 6)

    counts = jnp.sum(kbuf[:, :, :, length:, :].astype(jnp.float32), axis=(0, 1, 2))[:8]
    a = lax.broadcasted_iota(jnp.int32, (8, HD), 0)
    b = lax.broadcasted_iota(jnp.int32, (8, HD), 1)
    starts = jnp.sum(jnp.where(a == b, counts, 0.0), axis=0, keepdims=True)
    ends = jnp.sum(jnp.where(a == b + 1, counts, 0.0), axis=0, keepdims=True)
    lane = lax.broadcasted_iota(jnp.int32, (1, HD), 1)
    ends = jnp.where(lane == 7, float(CTX * length), ends)
    token = lax.broadcasted_iota(jnp.int32, (length, HD), 0).astype(jnp.float32)
    ones_at = (lane >= 8) & (lane < 11)
    ones_row = jnp.where(ones_at, 1.0, 0.0)
    ones_block = jnp.broadcast_to(ones_row, (length, HD)).astype(jnp.bfloat16)

    def extend(j, _):
        y, z, x = j // (NZ * NX), (j // NX) % NZ, j % NX
        lines = pl.ds(pl.multiple_of(j * length, length), length)
        first = (j * length).astype(jnp.float32)
        inside = (token >= starts - first) & (token < ends - first)
        kxe[lines, :HD] = kbuf[y, z, x, :length, :]
        kxe[lines, HD:] = jnp.where(inside, -BIG, ones_row).astype(jnp.bfloat16)
        vxe[lines, :HD] = vbuf[y, z, x]
        vxe[lines, HD:] = ones_block
        return 0

    lax.fori_loop(0, me + 1, extend, 0)
    other = jnp.where((row16 < 8) & (row16 != doc[...]), 1.0, 0.0)
    for h in range(heads):
        qx[h, HD : HD + 16, :] = other.astype(jnp.bfloat16)
    key_id = lax.broadcasted_iota(jnp.int32, (length, length), 0)
    query_id = lax.broadcasted_iota(jnp.int32, (length, length), 1)
    ones16 = jnp.ones((16, length), jnp.bfloat16)

    def forward(j, diagonal):
        lines = pl.ds(pl.multiple_of(j * length, length), length)
        key = kxe[lines, :]
        value_t = jnp.concatenate([vxe[lines, :HD].T, ones16], axis=0)
        tops, shrinks = [], []
        for h in range(heads):
            logits = dot(key, qx[h])
            if diagonal:
                logits = jnp.where(key_id <= query_id, logits, -BIG)
            sb[:, h * length : (h + 1) * length] = logits
            new = jnp.max(logits, axis=0, keepdims=True)
            if not diagonal:
                old = top[h]
                new = jnp.maximum(old, new)
                shrinks.append(jnp.exp2((old - new) * factor))
            top[h] = new
            tops.append(new * factor)
        for h in range(heads):
            cols = slice(h * length, (h + 1) * length)
            pb[:, cols] = jnp.exp2(sb[:, cols] * factor - tops[h]).astype(jnp.bfloat16)
        for h in range(heads):
            more = dot(value_t, pb[:, h * length : (h + 1) * length])
            ot[h] = more if diagonal else ot[h] * shrinks[h] + more

    def forward_step(i, _):
        forward(me - i, False)
        return 0

    def forward_part(k):
        lax.fori_loop(1 + me * k // 5, 1 + me * (k + 1) // 5, forward_step, 0)

    forward(me, True)
    forward_part(0)
    for part_ in expert_sums:
        part_.own(1)
        part_.far(2)
    forward_part(1)
    for part_ in expert_sums:
        part_.near(2)
    go(weights, 5)
    forward_part(2)
    for part_ in expert_sums:
        part_.own(2)
        part_.last()
    forward_part(3)

    routed_grad = jnp.concatenate([part_.total() for part_ in expert_sums], axis=1)
    hidden = hid[...].astype(jnp.float32)
    inverse = lax.rsqrt(
        fold_rows(jnp.sum(hidden * hidden, axis=1, keepdims=True)) * (1.0 / features) + EPS
    )
    normed = (hidden * inverse * gain16[...]).astype(jnp.bfloat16).astype(jnp.float32)
    score = jax.nn.sigmoid(fold_rows(jnp.sum(normed * column16[...], axis=1, keepdims=True)))
    dots = fold_rows(jnp.sum(routed_grad * normed, axis=1, keepdims=True))
    score_grad = dots * score * (1.0 - score)
    scaled = gain16[...] * (routed_grad * score + score_grad * column16[...])
    mean = fold_rows(jnp.sum(scaled * hidden, axis=1, keepdims=True)) * (1.0 / features)
    own_rows = inverse * scaled - hidden * (inverse * inverse * inverse) * mean
    rows[tp] = own_rows.astype(jnp.bfloat16)

    def swap(d, source):
        return remote(
            rows.at[source], rows.at[source], tsend.at[d], trecv.at[d], {"tp": (tp + d) % TP}
        )

    for d in range(1, TP):
        swap(d, tp).start()
    forward_part(4)

    for d in range(1, TP):
        swap(d, (tp + TP - d) % TP).wait_recv()

    for i in range(4):

        def add(t, _, i=i):
            cols = pl.ds(pl.multiple_of(t * 256, 256), 256)
            wide = pl.ds(pl.multiple_of(i * quarter + t * 256, 256), 256)
            more = dot(scat[i], rows[:, :, cols].reshape(TP * 16, 256))
            res[:, wide] = (og[:, wide].astype(jnp.float32) + more).astype(jnp.bfloat16)
            return 0

        lax.fori_loop(0, quarter // 256, add, 0)
    save_res = pltpu.make_async_copy(res, res_out, stores.at[5])
    save_res.start()

    go(weights, 6)
    acc[...] = jnp.zeros_like(acc)

    def project(i, _):
        y, z = i // 2, (i % 2) * 2
        left = res[:, pl.ds(pl.multiple_of(i * 640, 640), 640)]
        acc[:, :384] += dot(left, wabuf[y, pl.ds(z, 2)].reshape(640, 384))
        acc[:, 384:] += dot(left, wbbuf[y, pl.ds(z, 2)].reshape(640, 256))
        return 0

    lax.fori_loop(0, 8, project, 0)
    for h in range(heads):
        grad = acc[:, h * HD : (h + 1) * HD].astype(jnp.bfloat16)
        gs[h * length : (h + 1) * length, :] = grad
        grad_t = grad.T
        gx[h, :HD, :] = grad_t
        total = ot[h, HD : HD + 1, :]
        delta = jnp.sum(ot[h, :HD, :] * grad_t.astype(jnp.float32), axis=0, keepdims=True) / total
        high, middle, rest = split3(-delta)
        extra = jnp.where(row16 == 8, high, 0.0)
        extra = jnp.where(row16 == 9, middle, extra)
        extra = jnp.where(row16 == 10, rest, extra)
        gx[h, HD : HD + 16, :] = extra.astype(jnp.bfloat16)
        high, middle, rest = split3(-(top[h] + jnp.log2(total) * (1.0 / factor)))
        extra = jnp.where(row16 == 8, high, other)
        extra = jnp.where(row16 == 9, middle, extra)
        extra = jnp.where(row16 == 10, rest, extra)
        qx[h, HD : HD + 16, :] = extra.astype(jnp.bfloat16)

    def backward(j, diagonal):
        lines = pl.ds(pl.multiple_of(j * length, length), length)
        key = kxe[lines, :]
        key_t = kxe[lines, :HD].T
        value = vxe[lines, :]
        for h in range(heads):
            cols = slice(h * length, (h + 1) * length)
            logits = dot(key, qx[h])
            if diagonal:
                logits = jnp.where(key_id <= query_id, logits, -BIG)
            prob = jnp.exp2(logits * factor)
            lb[:, cols] = (prob * dot(value, gx[h])).astype(jnp.bfloat16)
            pb[:, cols] = prob.astype(jnp.bfloat16)
        value_sum = dot(pb[...], gs[...])
        key_sum = dot(lb[...], qs[...]) * scale
        for h in range(heads):
            more = dot(key_t, lb[:, h * length : (h + 1) * length])
            dqt[h] = dqt[h] + more
        y, z, x = j // (NZ * NX), (j // NX) % NZ, j % NX
        pk[y, z, x] = key_sum.astype(jnp.bfloat16)
        pv[y, z, x] = value_sum.astype(jnp.bfloat16)

    sums = [
        Share(pk, ak, ck, bk, None, 0, dsend.at[0], drecv.at[0]),
        Share(pv, av, cv, bv, None, 1, dsend.at[1], drecv.at[1]),
    ]
    y, z, x = place_of()
    for h in range(heads):
        dqt[h] = jnp.zeros((HD, length), jnp.float32)

    def backward_step(i, _):
        r = jnp.where(i < 14, i - 8, i - 14)
        turn = jnp.where(i < 14, r // 2, r // 6)
        to_y = (y + 3 - 2 * turn + turn // 2) % NY
        turn = (r % 6) // 2
        to_z = (z + 3 - 2 * turn + turn // 2) % NZ
        to_y = jnp.where(i < 8, (y + 2) % NY, to_y)
        to_z = jnp.where(i < 8, i // 2, jnp.where(i < 14, (z + 2) % NZ, to_z))
        j = to_y * (NZ * NX) + to_z * NX + i % 2

        @pl.when(j < me)
        def _():
            backward(j, False)

        @pl.when(j == me)
        def _():
            backward(j, True)

        @pl.when(j > me)
        def _():
            pk[to_y, to_z, i % 2] = jnp.zeros((length, HD), jnp.bfloat16)
            pv[to_y, to_z, i % 2] = jnp.zeros((length, HD), jnp.bfloat16)

        @pl.when(i == 7)
        def _():
            sums[0].far(1)

        @pl.when(i == 13)
        def _():
            sums[1].far(1)

        @pl.when(i == 25)
        def _():
            sums[0].near(1)

        @pl.when(i == 29)
        def _():
            sums[1].near(1)

        return 0

    lax.fori_loop(0, CTX, backward_step, 0)
    for part_ in sums:
        part_.own(1)
        part_.spread()
    for h in range(heads):
        dq[:, h * HD : (h + 1) * HD] = (dqt[h].T * scale).astype(jnp.bfloat16)
    dk[...] = sums[0].total().astype(jnp.bfloat16)
    dv[...] = sums[1].total().astype(jnp.bfloat16)
    for part_ in sums:
        part_.finish()

    for part_ in expert_sums:
        part_.finish()
    for d in range(1, TP):
        swap(d, tp).wait_send()
    for piece_ in moe + keys + weights:
        piece_.finish()
    for save in saves:
        save.wait()
    save_res.wait()


def fused(kin, v, wt, q, doc, eid, gain, column, gate, up, down, og, residual):
    length, width = q.shape
    heads = width // HD
    features = down.shape[1]
    rows = CTX * CAPL
    hidden = gate.shape[1]
    bf16, f32 = jnp.bfloat16, jnp.float32

    def shape(*dims):
        return jax.ShapeDtypeStruct(dims, bf16)

    vmem = pl.BlockSpec(memory_space=pltpu.VMEM)
    hbm = pl.BlockSpec(memory_space=pl.ANY)
    return pl.pallas_call(
        kernel,
        out_shape=[
            shape(length, features),
            shape(rows, features),
            shape(rows, features),
            shape(rows, hidden),
            shape(rows, hidden),
            shape(rows, hidden),
            shape(length, width),
            shape(length, HD),
            shape(length, HD),
        ],
        in_specs=[vmem] * 8 + [hbm] * 5,
        out_specs=[hbm] * 6 + [vmem] * 3,
        scratch_shapes=[
            pltpu.VMEM((NY, NZ, NX) + (16, features // 4), bf16),
            pltpu.VMEM((NY, NZ, NX) + (16, features // 4), bf16),
            pltpu.VMEM((NY, NZ, NX) + (length + 16, HD), bf16),
            pltpu.VMEM((NY, NZ, NX) + v.shape, bf16),
            pltpu.VMEM((NY, NZ, NX) + (wt.shape[0], 256), bf16),
            pltpu.VMEM((NY, NZ, NX) + (wt.shape[0], 384), bf16),
            pltpu.VMEM((2 * features, hidden), bf16),
            pltpu.VMEM((hidden, features), bf16),
            pltpu.VMEM((length, features), bf16),
            pltpu.VMEM((length, features), bf16),
            pltpu.VMEM((512, 512), bf16),
            pltpu.VMEM((512, 512), bf16),
            pltpu.VMEM((512, features // 4), bf16),
            pltpu.VMEM((rows, features), bf16),
            pltpu.VMEM((rows, features), bf16),
            pltpu.VMEM((rows, hidden), bf16),
            pltpu.VMEM((rows, hidden), bf16),
            pltpu.VMEM((rows, hidden), bf16),
            pltpu.VMEM((NY, NZ, NX, 16, features // 8), bf16),
            pltpu.VMEM((NY, NZ, NX, 16, features // 8), bf16),
            pltpu.VMEM((TP, 16, features // 4), bf16),
            pltpu.VMEM((CTX * length, 2 * HD), bf16),
            pltpu.VMEM((CTX * length, 2 * HD), bf16),
            pltpu.VMEM((heads, 2 * HD, length), bf16),
            pltpu.VMEM((heads, 2 * HD, length), bf16),
            pltpu.VMEM((heads, HD + 16, length), f32),
            pltpu.VMEM((heads, 1, length), f32),
            pltpu.VMEM((length, heads * length), f32),
            pltpu.VMEM((length, heads * length), bf16),
            pltpu.VMEM((length, heads * length), bf16),
            pltpu.VMEM((heads * length, HD), bf16),
            pltpu.VMEM((heads * length, HD), bf16),
            pltpu.VMEM((heads, HD, length), f32),
            pltpu.VMEM((length, width), f32),
            pltpu.VMEM((16, features // 4), bf16),
            pltpu.VMEM((16, features // 4), bf16),
            pltpu.VMEM((length + 16, HD), bf16),
            pltpu.VMEM((4, length, 64), bf16),
            pltpu.VMEM((16, features // 4), f32),
            pltpu.VMEM((16, features // 4), f32),
            pltpu.VMEM((NY, NZ, NX, length, HD), bf16),
            pltpu.VMEM((NY, NZ, NX, length, HD), bf16),
            pltpu.VMEM((2, 2, 2, length, HD), bf16),
            pltpu.VMEM((2, 4, 2, length, HD), bf16),
            pltpu.VMEM((8, length, HD), bf16),
            pltpu.VMEM((2, 2, 2, length, HD), bf16),
            pltpu.VMEM((2, 4, 2, length, HD), bf16),
            pltpu.VMEM((8, length, HD), bf16),
            pltpu.VMEM((2, 2, 2, 16, features // 8), bf16),
            pltpu.VMEM((2, 4, 2, 16, features // 8), bf16),
            pltpu.VMEM((3, 1, 16, features // 8), bf16),
            pltpu.VMEM((2, 2, 16, features // 8), bf16),
            pltpu.VMEM((2, 2, 2, 16, features // 8), bf16),
            pltpu.VMEM((2, 4, 2, 16, features // 8), bf16),
            pltpu.VMEM((3, 1, 16, features // 8), bf16),
            pltpu.VMEM((2, 2, 16, features // 8), bf16),
            pltpu.SemaphoreType.DMA((6, 9)),
            pltpu.SemaphoreType.DMA((6, 9)),
            pltpu.SemaphoreType.DMA((6,)),
            pltpu.SemaphoreType.DMA((2, 9)),
            pltpu.SemaphoreType.DMA((2, 9)),
            pltpu.SemaphoreType.DMA((TP,)),
            pltpu.SemaphoreType.DMA((TP,)),
            pltpu.SemaphoreType.DMA((2, 12)),
            pltpu.SemaphoreType.DMA((2, 12)),
            pltpu.SemaphoreType.DMA((5,)),
            pltpu.SemaphoreType.DMA((6,)),
        ],
        compiler_params=pltpu.CompilerParams(
            collective_id=1, has_side_effects=True, vmem_limit_bytes=60 << 20
        ),
    )(kin, v, wt, q, doc, eid, gain, column, gate, up, down, og, residual)


def local(
    residual,
    out_grad,
    queries,
    key_rows,
    value_rows,
    doc_ids,
    expert_ids,
    norm_gain,
    router_columns,
    gate_weight,
    up_weight,
    down_weight,
    out_weight,
):
    residual_grad, routed, grads, gate_delta, up_delta, active, query_grad, key_grad, value_grad = fused(
        key_rows,
        value_rows,
        out_weight.T,
        queries,
        doc_ids[None, :],
        expert_ids[None, :],
        norm_gain[None, :],
        router_columns.reshape(1, -1),
        gate_weight[0],
        up_weight[0],
        down_weight[0],
        out_grad,
        residual,
    )
    grad_gate = contract(routed, gate_delta, 0, 0).astype(jnp.bfloat16)
    grad_up = contract(routed, up_delta, 0, 0).astype(jnp.bfloat16)
    grad_down = contract(active, grads, 0, 0).astype(jnp.bfloat16)
    return (
        residual_grad, query_grad, key_grad, value_grad, grad_gate[None], grad_up[None], grad_down[None]
    )


def solution(mesh):
    in_specs = (
        P("ctx", None),
        P("ctx", None),
        P("ctx", "tp"),
        P("ctx", "tp"),
        P("ctx", "tp"),
        P("ctx"),
        P("ctx"),
        P(),
        P(None, "tp"),
        P("tp", None, "ctx"),
        P("tp", None, "ctx"),
        P("tp", "ctx", None),
        P("tp", "ctx"),
    )
    out_specs = (
        P("ctx", None),
        P("ctx", "tp"),
        P("ctx", "tp"),
        P("ctx", "tp"),
        P("tp", None, "ctx"),
        P("tp", None, "ctx"),
        P("tp", "ctx", None),
    )
    return jax.shard_map(local, mesh=mesh, in_specs=in_specs, out_specs=out_specs, check_vma=False)
```
